32 devices in a mesh: gx: 4 (over z), gy: 8 (over y, x, core).
Axes of the slice: x: 2, y: 2, z: 4, core: 2. Of those that a mesh axis runs over, the one named last changes fastest.
Arguments:
- control: float32 [4, 64, 64, 2048], P(None, None, 'gx', 'gy'), may hold values from -6 to 6
- background: float32 [4, 64, 64, 2048], P(None, None, 'gx', 'gy'), may hold values from -6 to 6
- vert_factor: float32 [4, 64, 64], replicated, may hold values from -0.75 to 0.75
- length_rates: float32 [2, 4, 64], replicated, may hold values from 0.5 to 40
- flash_weights: float32 [4, 64], replicated, may hold values from -3 to 3
- level_weights: float32 [64], replicated, may hold values from -0.75 to 0.75
- obs_owner: int32 [16384, 1], P(('gx', 'gy')), may hold values from 0 to 31; in each aligned block of 512 rows (0 to 511, 512 to 1023, ...) at most 32 rows name the same one
- obs_cell: int32 [16384], P(('gx', 'gy')), may hold values from 0 to 4095
- obs_count: int32 [32], P(('gx', 'gy')), may hold values from 256 to 512, as said below
- flash_obs: float32 [16384], P(('gx', 'gy')), may hold values from 0.1 to 3
- obs_error: float32 [16384], P(('gx', 'gy')), may hold values from 0.3 to 1
Outputs:
- grad: float32 [4, 64, 64, 2048], P(None, None, 'gx', 'gy')
- departure: float32 [16384], P(('gx', 'gy'))
The draws below stay inside these ranges and needn't reach their ends.
Inputs may be any that keep to these rules, and one draw needn't show every extreme that they name: `obs_owner`: among one device's 512 slots no owner is named more than 32 times, a bound that some block reaches. Only the first obs_count slots of a device are live; some device has all 512 live.
All inputs are finite; a program needn't handle non-finite values.
Results may differ from the reference program's by a relative error of at most 0.0003.
Values sent between devices are 32-bit elements; how exact they have to be, the bound alone decides.
A program may use at most 128 MiB of HBM per device.

```python
import math
import jax
import jax.numpy as jnp
import numpy as np
from jax import lax

NV = 4
LEV = 64
CX = 16
CY = 256
OBS_DEV = 512
NX = 64
NY = 2048
NOBS = 16384
CAP = 32
N_GX = 4
N_GY = 8
DEVICES = 32


def draw_obs_count(key, part):
    counts = jax.random.randint(key, (DEVICES,), OBS_DEV // 2, OBS_DEV + 1)
    fullest = jax.random.randint(jax.random.fold_in(key, 7), (), 0, DEVICES)
    return counts.at[fullest].set(OBS_DEV).astype(jnp.int32)


def with_ends(drawn, key, low, high):
    longest = drawn.shape.index(max(drawn.shape))
    spots = []
    for shift in (0, 1):
        where = [jax.random.randint(jax.random.fold_in(key, axis), (), 0, length) for axis, length in enumerate(drawn.shape)]
        where[longest] = (where[longest] + shift) % drawn.shape[longest]
        spots.append(tuple(where))
    return drawn.at[spots[0]].set(low).at[spots[1]].set(high)


def block_scale(key, shape, cuts, smallest, high):
    loudness, own = 1.0, jax.random.fold_in(key, 6)
    for dim, shards_of in cuts:
        draws = jnp.exp(jax.random.uniform(jax.random.fold_in(own, dim), (shards_of,), jnp.float32, smallest / len(cuts), high / len(cuts)))
        loudness = loudness * jnp.repeat(draws, shape[dim] // shards_of).reshape([-1 if axis == dim else 1 for axis in range(len(shape))])
    return loudness


def shared_out(stream_key, own, number, rows, number_of, top, most, lean):
    sequence = jax.random.permutation(stream_key, number_of)
    packed, common = load_shares(number_of, rows * top, most, lean, True), load_shares(number_of, rows * top, most, lean, False)
    places = jnp.arange(number_of)

    def named(tallies, rotation):
        used = int((tallies > 0).sum())
        fixed = max(1, used // 4)
        moved = fixed + (places - fixed + rotation * (used - fixed)) % max(1, number_of - fixed)
        return jnp.zeros((number_of,), jnp.int32).at[sequence[jnp.where(places < fixed, places, moved)]].set(jnp.asarray(tallies, jnp.int32))

    tallies = jnp.where(number % 4 == 0, named(packed, number // 4), named(common, number - number // 4 - 1))
    mixed = jax.random.permutation(jax.random.fold_in(own, 3), number_of)
    source_of, receiver = mixed[0:number_of // 2 * 2:2], mixed[1:number_of // 2 * 2:2]
    room = jnp.minimum(tallies[source_of] - 1, most - tallies[receiver]) // 2
    room = jnp.where((source_of == sequence[0]) | (receiver == sequence[0]) | (tallies[receiver] == 0), 0, jnp.maximum(room, 0))
    moved = jax.random.randint(jax.random.fold_in(own, 4), (number_of // 2,), 0, 1 << 20) % (room + 1)
    tallies = tallies.at[source_of].add(-moved).at[receiver].add(moved)
    members = jnp.searchsorted(jnp.cumsum(tallies), jnp.arange(rows * top), side="right").astype(jnp.int32)
    listing = members.reshape(top, rows).T
    listing = listing[jax.random.permutation(jax.random.fold_in(own, 1), rows)]
    rotation = jax.random.randint(jax.random.fold_in(own, 2), (rows, 1), 0, top)
    return jnp.take_along_axis(listing, (jnp.arange(top)[None, :] + rotation) % top, axis=1)


def load_shares(amount, total, limit, lean, full):
    loads = [(1 << 20) // math.isqrt(standing ** lean) + 1 for standing in range(1, amount + 1)]
    largest = limit if full else min(limit, max(-(-total // amount), total * loads[0] // sum(loads)))
    least = 1 if total - largest >= amount - 1 else 0
    holding, rest = [largest] + [least] * (amount - 1), total - largest - least * (amount - 1)
    while rest > 0:
        movable = [i for i in range(1, amount) if holding[i] < largest] or [i for i in range(1, amount) if holding[i] < limit]
        pool, left = sum([loads[i] for i in movable]), rest
        for i in movable:
            extra = min(limit - holding[i], max(1, left * loads[i] // pool), rest)
            holding[i] = holding[i] + extra
            rest = rest - extra
    return np.array(holding)


def gaussian(stream_key, shape, width, reach, cuts=(), dtype=jnp.bfloat16):
    array = jax.random.normal(stream_key, shape, jnp.float32) * width
    if len(cuts) > 0:
        array = block_scale(stream_key, shape, cuts, -0.22, 0.18) * array
    return jnp.clip(array, min=-reach, max=reach).astype(dtype)


def setup_inputs(seed: int = 0) -> dict:
    streams_of = jax.random.split(jax.random.key(seed), 12)
    control = gaussian(streams_of[0], (NV, LEV, NX, NY), 1.0, 6.0, ((2, 4), (3, 8)), jnp.float32)
    background = gaussian(streams_of[1], (NV, LEV, NX, NY), 1.0, 6.0, ((2, 4), (3, 8)), jnp.float32)
    vert_factor = gaussian(streams_of[2], (NV, LEV, LEV), LEV ** -0.5, 0.75, (), jnp.float32)
    length_rates = jnp.clip(jnp.exp(jax.random.uniform(streams_of[3], (2, NV, LEV), jnp.float32, math.log(0.5), math.log(40.0))), 0.5, 40.0)
    flash_weights = gaussian(streams_of[4], (NV, LEV), NV ** -0.5, 3.0, (), jnp.float32)
    level_weights = gaussian(streams_of[5], (LEV,), LEV ** -0.5, 0.75, (), jnp.float32)
    obs_owner_keys = jax.random.split(jax.random.fold_in(streams_of[6], 1), NOBS // OBS_DEV)
    obs_owner_turns = jax.random.permutation(jax.random.fold_in(streams_of[6], 3), NOBS // OBS_DEV)
    obs_owner = jax.vmap(lambda own, number: shared_out(jax.random.fold_in(streams_of[6], 2), own, number, OBS_DEV, N_GX * N_GY, 1, CAP, 2))(obs_owner_keys, obs_owner_turns).reshape((NOBS, 1))
    obs_cell = with_ends(jax.random.randint(streams_of[7], (NOBS,), 0, CX * CY), jax.random.fold_in(streams_of[7], 1), 0, (CX * CY) - 1).astype(jnp.int32)
    obs_count = draw_obs_count(jax.random.fold_in(streams_of[11], 71), 0)
    flash_obs = jnp.clip(jnp.exp(math.log(3.0) - 3.4011974 * jax.random.uniform(streams_of[9], (NOBS,), jnp.float32) ** block_scale(streams_of[9], (NOBS,), ((0, 32),), -0.2, 0.2)), 0.1, 3.0)
    obs_error = jnp.clip(jnp.exp(math.log(1.0) - 1.2039728 * jax.random.uniform(streams_of[10], (NOBS,), jnp.float32) ** block_scale(streams_of[10], (NOBS,), ((0, 32),), -0.2, 0.2)), 0.3, 1.0)
    return dict(control=control, background=background, vert_factor=vert_factor, length_rates=length_rates, flash_weights=flash_weights, level_weights=level_weights, obs_owner=obs_owner, obs_cell=obs_cell, obs_count=obs_count, flash_obs=flash_obs, obs_error=obs_error)


highest = lax.Precision.HIGHEST

def recursive_pass(field, step, axis, reverse):
    decay = jnp.exp(-step)[:, :, None]
    gain = jnp.sqrt(-jnp.expm1(-2.0 * step))[:, :, None]
    moved = jnp.moveaxis(field, axis, 0)

    def advance(carry, column):
        carry = decay * carry + gain * column
        return (carry, carry)
    start = jnp.zeros(moved.shape[1:], jnp.float32)
    _, result = lax.scan(advance, start, moved, reverse=reverse)
    return jnp.moveaxis(result, 0, axis)

def observe(columns, flash, sigma, flash_weights, level_weights):
    levels = jnp.einsum('nvk,vk->nk', columns, flash_weights, precision=highest)
    total = jnp.dot(jax.nn.softplus(levels), level_weights, precision=highest)
    miss = jax.nn.softplus(total) - flash
    weight = miss / (sigma * sigma) * jax.nn.sigmoid(total)
    adjoint = weight[:, None, None] * (level_weights[None, :] * jax.nn.sigmoid(levels))[:, None, :] * flash_weights[None]
    return (miss, adjoint)

def reference(control, background, vert_factor, length_rates, flash_weights, level_weights, obs_owner, obs_cell, obs_count, flash_obs, obs_error):
    step_x = length_rates[0] / NX
    step_y = length_rates[1] / NY
    smooth = recursive_pass(recursive_pass(control, step_y, 3, False), step_x, 2, False)
    state = background + jnp.einsum('vkj,vjxy->vkxy', vert_factor, smooth, precision=highest)
    owner = obs_owner[:, 0]
    row_index = owner // N_GY * CX + obs_cell // CY
    col_index = owner % N_GY * CY + obs_cell % CY
    slots = jnp.arange(NOBS).astype(jnp.int32)
    live = slots % OBS_DEV < jnp.repeat(obs_count, OBS_DEV)
    livef = live.astype(jnp.float32)
    columns = jnp.transpose(state[:, :, row_index, col_index], (2, 0, 1))
    miss, adjoint = observe(columns, flash_obs, obs_error, flash_weights, level_weights)
    departure = miss * livef
    adjoint = adjoint * livef[:, None, None]
    forcing = jnp.zeros_like(state).at[:, :, row_index, col_index].add(jnp.transpose(adjoint, (1, 2, 0)))
    back = jnp.einsum('vjk,vjxy->vkxy', vert_factor, forcing, precision=highest)
    grad = control + recursive_pass(recursive_pass(back, step_x, 2, True), step_y, 3, True)
    return (grad, departure)
```

```python
import functools
import jax
import jax.numpy as jnp
from jax import lax
from jax.experimental import pallas as pl
from jax.experimental.pallas import tpu as pltpu
from jax.sharding import PartitionSpec as P

LANES = 128
MESH = pl.DeviceIdType.MESH
f32, bf16 = jnp.float32, jnp.bfloat16


def split(value):
    high = value.astype(bf16)
    return high, (value - high.astype(f32)).astype(bf16)


def dot(left, right):
    return jnp.dot(left, right, preferred_element_type=f32)


def kernel(
    nx, ny, variables, levels, rx, ry,
    ctrl, bg, tab, lwt, forward, backward, obs, seen,
    out, dep,
    field, sums, sp_all, obs_all, edge, edge_b, q_ref, xin, xout, xin_b, xout_b, row0, axt, stage, base_levels, mstack, bstack,
    obs_s, obs_r, sp_s, sp_r, e_s, e_r, f_s, f_r, x_s, x_r, b_s, b_r,
):
    devices = nx * ny
    gx, gy = lax.axis_index("gx"), lax.axis_index("gy")
    me = gx * ny + gy
    halves = ry // LANES
    tiles = levels // 8
    vk = variables * levels
    lane = lax.broadcasted_iota(jnp.int32, (8, LANES), 1)
    lane_f = lane.astype(f32)
    shifts = [1 << s for s in range(7)]

    def peer(offset):
        other = lax.rem(me + offset, devices)
        return (other // ny, lax.rem(other, ny))

    def to_all(ref, send, recv):
        def one(offset):
            return pltpu.make_async_remote_copy(
                ref.at[me], ref.at[me], send.at[offset], recv.at[me], peer(offset), MESH
            )
        return one

    def from_all(ref, send, recv, offset):
        src = lax.rem(me + offset, devices)
        return pltpu.make_async_remote_copy(
            ref.at[src], ref.at[src], send.at[offset], recv.at[src], peer(offset), MESH
        )

    def start_all(ref, send, recv):
        @pl.loop(1, devices)
        def _(offset):
            to_all(ref, send, recv)(offset).start()

    def wait_all(ref, send, recv):
        @pl.loop(1, devices)
        def _(offset):
            from_all(ref, send, recv, offset).wait_recv()
            to_all(ref, send, recv)(offset).wait_send()

    def row_copy(ref, send, recv, offset, slot):
        other = lax.rem(gy + offset, ny)
        return pltpu.make_async_remote_copy(
            ref.at[slot], ref.at[slot], send.at[offset], recv.at[slot], (gx, other), MESH
        )

    def start_row(ref, send, recv):
        @pl.loop(1, ny)
        def _(offset):
            row_copy(ref, send, recv, offset, gy).start()

    def wait_row(ref, send, recv):
        @pl.loop(1, ny)
        def _(offset):
            row_copy(ref, send, recv, offset, lax.rem(gy + offset, ny)).wait_recv()
            row_copy(ref, send, recv, offset, gy).wait_send()

    def chain(v, source, target, send, recv, other):
        return pltpu.make_async_remote_copy(
            source.at[v], target.at[v], send.at[v], recv.at[v], (other, gy), MESH
        )

    def half(h):
        return slice(h * LANES, (h + 1) * LANES)

    def rates(v, tile):
        rows = pl.ds(tile * 8, 8)
        return tab[v, rows, :], tab[variables + v, rows, :]

    def scan_y(parts, coefs, reach, reverse):
        done = [None] * halves
        carry = None
        for h in (range(halves)[::-1] if reverse else range(halves)):
            part = parts[h]
            for s, c in zip(shifts, coefs):
                part = part + c * pltpu.roll(part, LANES - s if reverse else s, 1)
            if carry is not None:
                part = part + reach * carry
            end = part[:, :1] if reverse else part[:, LANES - 1:]
            carry = jnp.broadcast_to(end, part.shape)
            done[h] = part
        return done, carry

    def forward_coefs(sy):
        return [jnp.where(lane >= s, jnp.exp(-sy * s), 0.0) for s in shifts]

    def backward_coefs(sy):
        return [jnp.where(lane < LANES - s, jnp.exp(-sy * s), 0.0) for s in shifts]

    barrier = pltpu.get_barrier_semaphore()

    @pl.loop(1, devices)
    def _(offset):
        pl.semaphore_signal(barrier, inc=1, device_id=peer(offset), device_id_type=MESH)
    pl.semaphore_wait(barrier, devices - 1)

    obs_all[me] = obs[...]
    start_all(obs_all, obs_s, obs_r)

    high, low = split(forward[...])
    mstack[...] = jnp.concatenate([high, low], axis=0)
    high, low = split(backward[...])
    bstack[...] = jnp.concatenate([high, high, low], axis=1)

    edge[gy] = jnp.zeros((levels, LANES), f32)
    edge_b[gy] = jnp.zeros((levels, LANES), f32)

    @pl.loop(0, variables * tiles)
    def _(i):
        v, tile = i // tiles, lax.rem(i, tiles)
        sx, sy = rates(v, tile)
        coefs = forward_coefs(sy)
        reach = jnp.exp(-sy * (lane_f + 1.0))
        ax = jnp.exp(-sx)
        axt[pl.ds(i * 8, 8), :] = ax
        for h in range(halves):
            stage[h] = ctrl[v, pl.ds(tile * 8 * rx, 8 * rx), half(h)]
        state = [jnp.zeros((8, LANES), f32)] * halves
        column = edge[gy, pl.ds(tile * 8, 8), :]
        for x in range(rx):
            parts = [stage[h, pl.ds(x, 8, stride=rx), :] for h in range(halves)]
            parts, last = scan_y(parts, coefs, reach, False)
            column = jnp.where(lane == v * rx + x, last, column)
            for h in range(halves):
                state[h] = ax * state[h] + parts[h]
                field[x, pl.ds(i * 8, 8), half(h)] = state[h]
        edge[gy, pl.ds(tile * 8, 8), :] = column

    start_row(edge, e_s, e_r)

    @pl.loop(0, tiles)
    def _(tile):
        for v in range(variables):
            for h in range(halves):
                stage[v * halves + h] = bg[v, pl.ds(tile * 8 * rx, 8 * rx), half(h)]
        weights = [tab[2 * variables + v, pl.ds(tile * 8, 8), :] for v in range(variables)]
        for x in range(rx):
            for h in range(halves):
                part = jnp.zeros((8, LANES), f32)
                for v in range(variables):
                    part = part + weights[v] * stage[v * halves + h, pl.ds(x, 8, stride=rx), :]
                base_levels[x, pl.ds(tile * 8, 8), half(h)] = part

    wait_all(obs_all, obs_s, obs_r)
    sums[...] = jnp.zeros_like(sums)
    per = obs.shape[1]
    row_x = lax.broadcasted_iota(jnp.int32, (rx, per), 0).astype(f32)
    row_y = lax.broadcasted_iota(jnp.int32, (ry, per), 0).astype(f32)
    base = (me * rx).astype(f32)

    @pl.loop(0, devices)
    def _(src):
        total = sums[...]
        for part in range(2):
            key = obs_all[src, part:part + 1, :] - base
            spot = obs_all[src, 2 + part:3 + part, :]
            hit = row_x == key
            pieces = []
            for field_of in (4, 6):
                weight = obs_all[src, field_of + part:field_of + part + 1, :]
                pieces += split(jnp.where(hit, weight, 0.0))
            left = jnp.concatenate(pieces, axis=0)
            right = jnp.where(row_y == spot, 1.0, 0.0).astype(bf16)
            total = total + lax.dot_general(
                left, right, (((1,), (1,)), ((), ())), preferred_element_type=f32
            )
        sums[...] = total

    @pl.when(gx == 0)
    def _():
        xin[...] = jnp.zeros_like(xin)

    @pl.when(gx == nx - 1)
    def _():
        xin_b[...] = jnp.zeros_like(xin_b)

    def rates_in_lanes(tile):
        wide = [jnp.zeros((8, LANES), f32)] * 2
        for v in range(variables):
            here = (lane >= v * rx) & (lane < (v + 1) * rx)
            wide = [jnp.where(here, new, old) for new, old in zip(rates(v, tile), wide)]
        return wide

    wait_row(edge, e_s, e_r)

    @pl.loop(0, tiles)
    def _(tile):
        rows = pl.ds(tile * 8, 8)
        sx, sy = rates_in_lanes(tile)
        total = jnp.zeros((8, LANES), f32)
        for src in range(ny):
            far = jnp.maximum(gy - 1 - src, 0).astype(f32) * ry
            total = total + jnp.where(src < gy, jnp.exp(-sy * far) * edge[src, rows, :], 0.0)
        inner = lax.rem(lane, rx)
        s = 1
        while s < rx:
            total = total + jnp.where(inner >= s, jnp.exp(-sx * s), 0.0) * pltpu.roll(total, s, 1)
            s *= 2
        q_ref[rows, :] = total

    for v in range(variables):
        @pl.when(gx > 0)
        def _():
            chain(v, xout, xin, x_s, x_r, gx).wait_recv()

        @pl.when(gx < nx - 1)
        def _():
            @pl.loop(0, tiles)
            def _(tile):
                rows = pl.ds(tile * 8, 8)
                sx, sy = rates(v, tile)
                spot = v * rx + rx - 1
                q = jnp.broadcast_to(q_ref[rows, spot:spot + 1], (8, LANES))
                for h in range(halves):
                    xout[v, rows, half(h)] = (
                        field[rx - 1, pl.ds(v * levels + tile * 8, 8), half(h)]
                        + jnp.exp(-sy * (lane_f + (1.0 + h * LANES))) * q
                        + jnp.exp(-sx * rx) * xin[v, rows, half(h)]
                    )
            chain(v, xout, xin, x_s, x_r, gx + 1).start()

        @pl.loop(0, tiles)
        def _(tile):
            rows = pl.ds(tile * 8, 8)
            sx, sy = rates(v, tile)
            reach = [jnp.exp(-sy * (lane_f + (1.0 + h * LANES))) for h in range(halves)]
            q_all = q_ref[rows, :]
            ax = jnp.exp(-sx)
            entering = [xin[v, rows, half(h)] for h in range(halves)]
            for x in range(rx):
                q = jnp.broadcast_to(q_all[:, v * rx + x:v * rx + x + 1], (8, LANES))
                for h in range(halves):
                    entering[h] = ax * entering[h]
                    at = (x, pl.ds(v * levels + tile * 8, 8), half(h))
                    field[at] = field[at] + reach[h] * q + entering[h]

    row0[...] = jnp.zeros_like(row0)
    wide = lambda value: jnp.concatenate([value] * halves, axis=1)

    @pl.loop(0, rx)
    def _(i):
        x = rx - 1 - i
        high, low = split(field[x])
        both = dot(mstack[...], high)
        value = both[:levels] + both[levels:] + dot(mstack[:levels, :], low)
        value = value + base_levels[x]
        small = jnp.exp(-jnp.abs(value))
        soft = jnp.maximum(value, 0.0) + jnp.log1p(small)
        slope = jnp.where(value >= 0, 1.0, small) / (1.0 + small)
        total = jnp.sum(wide(lwt[...]) * soft, axis=0, keepdims=True)
        small = jnp.exp(-jnp.abs(total))
        sp = jnp.maximum(total, 0.0) + jnp.log1p(small)
        sg = jnp.where(total >= 0, 1.0, small) / (1.0 + small)
        sp_all[me, pl.ds(x, 1), :] = sp
        s1 = sums[pl.ds(x, 1), :] + sums[pl.ds(rx + x, 1), :]
        s2 = sums[pl.ds(2 * rx + x, 1), :] + sums[pl.ds(3 * rx + x, 1), :]
        high, low = split(sg * (sp * s1 - s2) * slope)
        back = dot(bstack[...], jnp.concatenate([high, low, high], axis=0))
        now = wide(axt[...]) * row0[...] + back
        row0[...] = now
        field[x] = now

    start_all(sp_all, sp_s, sp_r)

    for v in range(variables):
        @pl.loop(0, tiles)
        def _(tile):
            sx, sy = rates(v, tile)
            coefs = backward_coefs(sy)
            reach = jnp.exp(-sy * (LANES - lane_f))
            for x in range(rx):
                rows = pl.ds(v * levels + tile * 8, 8)
                parts = [field[x, rows, half(h)] for h in range(halves)]
                parts, _ = scan_y(parts, coefs, reach, True)
                for h in range(halves):
                    field[x, rows, half(h)] = parts[h]

        @pl.when(gx < nx - 1)
        def _():
            chain(v, xout_b, xin_b, b_s, b_r, gx).wait_recv()

        @pl.when(gx > 0)
        def _():
            xout_b[v] = row0[v * levels:(v + 1) * levels, :] + wide(
                jnp.exp(-tab[v] * rx)
            ) * xin_b[v]
            chain(v, xout_b, xin_b, b_s, b_r, gx - 1).start()

        @pl.loop(0, tiles)
        def _(tile):
            rows = pl.ds(tile * 8, 8)
            sx, sy = rates(v, tile)
            parts = [xin_b[v, rows, half(h)] for h in range(halves)]
            parts, first = scan_y(
                parts, backward_coefs(sy), jnp.exp(-sy * (LANES - lane_f)), True
            )
            for h in range(halves):
                row0[pl.ds(v * levels + tile * 8, 8), half(h)] = parts[h]
            column = edge_b[gy, rows, :]
            for x in range(rx):
                own = field[x, pl.ds(v * levels + tile * 8, 8), :LANES][:, :1]
                whole = jnp.broadcast_to(own, (8, LANES)) + jnp.exp(-sx * (rx - x)) * first
                column = jnp.where(lane == v * rx + x, whole, column)
            edge_b[gy, rows, :] = column

    start_row(edge_b, f_s, f_r)

    wait_all(sp_all, sp_s, sp_r)
    count = seen.shape[1]
    key, flash = seen[0:1, :], seen[2:3, :]
    column_y = lax.broadcasted_iota(jnp.int32, (ry, count), 0).astype(f32)
    pick = jnp.where(column_y == seen[1:2, :], 1.0, 0.0).astype(bf16)
    row_of = lax.broadcasted_iota(jnp.int32, (rx, count), 0).astype(f32)

    def find(src, found):
        high, low = split(sp_all[src])
        value = dot(jnp.concatenate([high, low], axis=0), pick)
        value = value[:rx] + value[rx:]
        return found + jnp.where(row_of == key - (src * rx).astype(f32), value, 0.0)

    found = lax.fori_loop(0, devices, find, jnp.zeros((rx, count), f32))
    found = jnp.sum(found, axis=0, keepdims=True)
    dep[...] = jnp.where(key >= 0, found - flash, 0.0)

    wait_row(edge_b, f_s, f_r)

    @pl.loop(0, tiles)
    def _(tile):
        rows = pl.ds(tile * 8, 8)
        sx, sy = rates_in_lanes(tile)
        total = jnp.zeros((8, LANES), f32)
        for src in range(ny):
            far = jnp.maximum(src - gy - 1, 0).astype(f32) * ry
            total = total + jnp.where(src > gy, jnp.exp(-sy * far) * edge_b[src, rows, :], 0.0)
        for v in range(variables):
            sx, sy = rates(v, tile)
            reach = [jnp.exp(-sy * (ry - h * LANES - lane_f)) for h in range(halves)]
            ax = jnp.exp(-sx)
            mine = pl.ds(v * levels + tile * 8, 8)
            entering = [row0[mine, half(h)] for h in range(halves)]
            for x in range(rx)[::-1]:
                q = jnp.broadcast_to(total[:, v * rx + x:v * rx + x + 1], (8, LANES))
                for h in range(halves):
                    entering[h] = ax * entering[h]
                    stage[v * halves + h, pl.ds(x, 8, stride=rx), :] = (
                        field[x, mine, half(h)] + reach[h] * q + entering[h]
                    )
            for h in range(halves):
                at = (v, pl.ds(tile * 8 * rx, 8 * rx), half(h))
                out[at] = ctrl[at] + stage[v * halves + h]

    for v in range(variables):
        @pl.when(gx < nx - 1)
        def _():
            chain(v, xout, xin, x_s, x_r, gx + 1).wait_send()

        @pl.when(gx > 0)
        def _():
            chain(v, xout_b, xin_b, b_s, b_r, gx - 1).wait_send()


def body(
    control, background, vert_factor, length_rates, flash_weights, level_weights,
    obs_owner, obs_cell, obs_count, flash_obs, obs_error,
):
    variables, levels, rx, ry = control.shape
    nx, ny = lax.axis_size("gx"), lax.axis_size("gy")
    devices = nx * ny
    count = obs_cell.shape[0]
    vk = variables * levels
    step_x = length_rates[0] / (rx * nx)
    step_y = length_rates[1] / (ry * ny)
    gain = jnp.sqrt(jnp.expm1(-2.0 * step_x) * jnp.expm1(-2.0 * step_y))
    forward = flash_weights[:, :, None] * vert_factor * gain[:, None, :]
    forward = forward.transpose(1, 0, 2).reshape(levels, vk)
    backward = (flash_weights * level_weights)[:, :, None] * vert_factor * gain[:, None, :]
    backward = backward.transpose(0, 2, 1).reshape(vk, levels)
    tab = jnp.concatenate([step_x, step_y, flash_weights], axis=0)
    tab = jnp.broadcast_to(tab[:, :, None], (3 * variables, levels, LANES))
    lwt = jnp.broadcast_to(level_weights[:, None], (levels, LANES))

    live = jnp.arange(count) < obs_count[0]
    key = jnp.where(live, obs_owner[:, 0] * rx + obs_cell // ry, -1).astype(f32)
    spot = (obs_cell % ry).astype(f32)
    weight = 1.0 / (obs_error * obs_error)
    obs = jnp.stack([key, spot, weight, flash_obs * weight]).reshape(8, count // 2)
    zero = jnp.zeros_like(key)
    seen = jnp.stack([key, spot, flash_obs, zero, zero, zero, zero, zero])

    vmem = pl.BlockSpec(memory_space=pltpu.VMEM)
    dma = pltpu.SemaphoreType.DMA
    grad, departure = pl.pallas_call(
        functools.partial(kernel, nx, ny, variables, levels, rx, ry),
        out_shape=(
            jax.ShapeDtypeStruct((variables, levels * rx, ry), f32),
            jax.ShapeDtypeStruct((1, count), f32),
        ),
        in_specs=[vmem] * 8,
        out_specs=(vmem, vmem),
        scratch_shapes=[
            pltpu.VMEM((rx, vk, ry), f32),
            pltpu.VMEM((4 * rx, ry), f32),
            pltpu.VMEM((devices, rx, ry), f32),
            pltpu.VMEM((devices, 8, count // 2), f32),
            pltpu.VMEM((ny, levels, LANES), f32),
            pltpu.VMEM((ny, levels, LANES), f32),
            pltpu.VMEM((levels, LANES), f32),
            pltpu.VMEM((variables, levels, ry), f32),
            pltpu.VMEM((variables, levels, ry), f32),
            pltpu.VMEM((variables, levels, ry), f32),
            pltpu.VMEM((variables, levels, ry), f32),
            pltpu.VMEM((vk, ry), f32),
            pltpu.VMEM((vk, LANES), f32),
            pltpu.VMEM((variables * ry // LANES, 8 * rx, LANES), f32),
            pltpu.VMEM((rx, levels, ry), f32),
            pltpu.VMEM((2 * levels, vk), bf16),
            pltpu.VMEM((vk, 3 * levels), bf16),
            dma((devices,)), dma((devices,)), dma((devices,)), dma((devices,)),
            dma((ny,)), dma((ny,)), dma((ny,)), dma((ny,)),
            dma((variables,)), dma((variables,)), dma((variables,)), dma((variables,)),
        ],
        compiler_params=pltpu.CompilerParams(
            collective_id=0, has_side_effects=True, vmem_limit_bytes=48 * 2**20
        ),
    )(
        control.reshape(variables, levels * rx, ry),
        background.reshape(variables, levels * rx, ry),
        tab, lwt, forward, backward, obs, seen,
    )
    return grad.reshape(control.shape), departure.reshape(count)


def solution(mesh):
    placed = (
        P(None, None, "gx", "gy"),
        P(None, None, "gx", "gy"),
        P(),
        P(),
        P(),
        P(),
        P(("gx", "gy"), None),
        P(("gx", "gy")),
        P(("gx", "gy")),
        P(("gx", "gy")),
        P(("gx", "gy")),
    )
    return jax.shard_map(
        body,
        mesh=mesh,
        in_specs=placed,
        out_specs=(P(None, None, "gx", "gy"), P(("gx", "gy"))),
        check_vma=False,
    )
```

```python
import functools
import jax
import jax.numpy as jnp
from jax import lax
from jax.experimental import pallas as pl
from jax.experimental.pallas import tpu as pltpu
from jax.sharding import PartitionSpec as P

LANES = 128
MESH = pl.DeviceIdType.MESH
f32, bf16 = jnp.float32, jnp.bfloat16


def split(value):
    high = value.astype(bf16)
    return high, (value - high.astype(f32)).astype(bf16)


def dot(left, right):
    return jnp.dot(left, right, preferred_element_type=f32)


def kernel(
    nx, ny, variables, levels, rx, ry,
    ctrl, bg, vert, rate, gain, flash_w, level_w, seen,
    out, dep,
    field, sums, sp_all, obs_all, edge, edge_b, q_ref, xin, xout, xin_b, xout_b, row0, axt, stage,
    base_levels, mstack, bstack, tab, raw, tri, tri_b, grow, fade, slopes, totals,
    obs_s, obs_r, sp_s, sp_r, e_s, e_r, f_s, f_r, x_s, x_r, b_s, b_r,
):
    devices = nx * ny
    gx, gy = lax.axis_index("gx"), lax.axis_index("gy")
    me = gx * ny + gy
    halves = ry // LANES
    tiles = levels // 8
    vk = variables * levels
    lane = lax.broadcasted_iota(jnp.int32, (8, LANES), 1)
    def peer(offset):
        other = lax.rem(me + offset, devices)
        return (other // ny, lax.rem(other, ny))

    def to_all(ref, send, recv):
        def one(offset):
            return pltpu.make_async_remote_copy(
                ref.at[me], ref.at[me], send.at[offset], recv.at[me], peer(offset), MESH
            )
        return one

    def from_all(ref, send, recv, offset):
        src = lax.rem(me + offset, devices)
        return pltpu.make_async_remote_copy(
            ref.at[src], ref.at[src], send.at[offset], recv.at[src], peer(offset), MESH
        )

    def start_all(ref, send, recv):
        @pl.loop(1, devices)
        def _(offset):
            to_all(ref, send, recv)(offset).start()

    def wait_all(ref, send, recv):
        @pl.loop(1, devices)
        def _(offset):
            from_all(ref, send, recv, offset).wait_recv()
            to_all(ref, send, recv)(offset).wait_send()

    def row_copy(ref, send, recv, offset, slot):
        other = lax.rem(gy + offset, ny)
        return pltpu.make_async_remote_copy(
            ref.at[slot], ref.at[slot], send.at[offset], recv.at[slot], (gx, other), MESH
        )

    def start_row(ref, send, recv):
        @pl.loop(1, ny)
        def _(offset):
            row_copy(ref, send, recv, offset, gy).start()

    def wait_row(ref, send, recv):
        @pl.loop(1, ny)
        def _(offset):
            row_copy(ref, send, recv, offset, lax.rem(gy + offset, ny)).wait_recv()
            row_copy(ref, send, recv, offset, gy).wait_send()

    def chain(v, source, target, send, recv, other):
        return pltpu.make_async_remote_copy(
            source.at[v], target.at[v], send.at[v], recv.at[v], (other, gy), MESH
        )

    def half(h):
        return slice(h * LANES, (h + 1) * LANES)

    def rates(v, tile):
        rows = pl.ds(tile * 8, 8)
        return tab[v, rows, :], tab[variables + v, rows, :]

    barrier = pltpu.get_barrier_semaphore()

    @pl.loop(1, devices)
    def _(offset):
        pl.semaphore_signal(barrier, inc=1, device_id=peer(offset), device_id_type=MESH)
    pl.semaphore_wait(barrier, devices - 1)

    count = seen.shape[1]
    per = count // 2
    cell_x = jnp.floor(seen[1:2, :] * (1.0 / ry))
    cell_y = seen[1:2, :] - cell_x * ry
    place = lax.broadcasted_iota(jnp.int32, (1, count), 1).astype(f32)
    key = jnp.where(place < seen[4:5, :], seen[0:1, :] * rx + cell_x, -1.0)
    flash = seen[2:3, :]
    weight = 1.0 / (seen[3:4, :] * seen[3:4, :])
    for number, value in enumerate((key, cell_y, weight, flash * weight)):
        for part in range(2):
            obs_all[me, 2 * number + part:2 * number + part + 1, :] = value[
                :, part * per:(part + 1) * per
            ]
    start_all(obs_all, obs_s, obs_r)

    raw[...] = jnp.zeros_like(raw)
    raw[:variables, :levels] = rate[0] * (1.0 / (rx * nx))
    raw[variables:2 * variables, :levels] = rate[1] * (1.0 / (ry * ny))
    raw[2 * variables:3 * variables, :levels] = flash_w[...]
    raw[3 * variables:3 * variables + 1, :levels] = level_w[...]
    turned = raw[...].T
    for c in range(3 * variables + 1):
        tab[c] = jnp.broadcast_to(turned[:levels, c:c + 1], (levels, LANES))

    for v in range(variables):
        mine = slice(v * levels, (v + 1) * levels)
        scaled = vert[v] * gain[v:v + 1, :] * tab[2 * variables + v, :, :levels]
        high, low = split(scaled)
        mstack[:levels, mine] = high
        mstack[levels:, mine] = low
        high, low = split((scaled * tab[3 * variables, :, :levels]).T)
        bstack[mine, :levels] = high
        bstack[mine, levels:2 * levels] = high
        bstack[mine, 2 * levels:] = low
    down = lax.broadcasted_iota(jnp.int32, (ry, ry), 0)
    across = lax.broadcasted_iota(jnp.int32, (ry, ry), 1)
    tri[...] = jnp.where(down <= across, 1.0, 0.0).astype(bf16)
    tri_b[...] = jnp.where(down >= across, 1.0, 0.0).astype(bf16)

    def prefix(value, triangle):
        high, low = split(value)
        both = dot(jnp.concatenate([high, low], axis=0), triangle[...])
        return both[:value.shape[0]] + both[value.shape[0]:]

    wide = lambda value: jnp.concatenate([value] * halves, axis=1)
    position = lax.broadcasted_iota(jnp.int32, (8, ry), 1).astype(f32)

    edge[gy] = jnp.zeros((levels, LANES), f32)
    edge_b[gy] = jnp.zeros((levels, LANES), f32)

    @pl.loop(0, variables * tiles, unroll=2)
    def _(i):
        v, tile = i // tiles, lax.rem(i, tiles)
        rows = pl.ds(i * 8, 8)
        sx, sy = rates(v, tile)
        up, fall = jnp.exp(wide(sy) * position), jnp.exp(-wide(sy) * position)
        grow[rows, :], fade[rows, :] = up, fall
        ax = jnp.exp(-sx)
        axt[rows, :] = ax
        ax = wide(ax)
        for h in range(halves):
            stage[v * halves + h] = ctrl[v, pl.ds(tile * 8 * rx, 8 * rx), half(h)]
        parts = [
            jnp.concatenate(
                [stage[v * halves + h, pl.ds(x, 8, stride=rx), :] for h in range(halves)], axis=1
            ) * up
            for x in range(rx)
        ]
        parts = prefix(jnp.concatenate(parts, axis=0), tri)
        state = jnp.zeros((8, ry), f32)
        column = edge[gy, pl.ds(tile * 8, 8), :]
        for x in range(rx):
            part = parts[x * 8:x * 8 + 8] * fall
            last = jnp.broadcast_to(part[:, ry - 1:], (8, LANES))
            column = jnp.where(lane == v * rx + x, last, column)
            state = ax * state + part
            field[x, rows, :] = state
        edge[gy, pl.ds(tile * 8, 8), :] = column

    start_row(edge, e_s, e_r)

    @pl.loop(0, tiles)
    def _(tile):
        for v in range(variables):
            for h in range(halves):
                stage[v * halves + h] = bg[v, pl.ds(tile * 8 * rx, 8 * rx), half(h)]
        weights = [tab[2 * variables + v, pl.ds(tile * 8, 8), :] for v in range(variables)]
        for x in range(rx):
            for h in range(halves):
                part = jnp.zeros((8, LANES), f32)
                for v in range(variables):
                    part = part + weights[v] * stage[v * halves + h, pl.ds(x, 8, stride=rx), :]
                base_levels[x, pl.ds(tile * 8, 8), half(h)] = part

    wait_all(obs_all, obs_s, obs_r)
    sums[...] = jnp.zeros_like(sums)
    row_x = lax.broadcasted_iota(jnp.int32, (rx, per), 0).astype(f32)
    row_y = lax.broadcasted_iota(jnp.int32, (ry, per), 0).astype(f32)
    base = (me * rx).astype(f32)

    @pl.loop(0, devices, unroll=2)
    def _(src):
        total = sums[...]
        for part in range(2):
            key = obs_all[src, part:part + 1, :] - base
            spot = obs_all[src, 2 + part:3 + part, :]
            hit = row_x == key
            pieces = []
            for field_of in (4, 6):
                weight = obs_all[src, field_of + part:field_of + part + 1, :]
                pieces += split(jnp.where(hit, weight, 0.0))
            left = jnp.concatenate(pieces, axis=0)
            right = jnp.where(row_y == spot, 1.0, 0.0).astype(bf16)
            total = total + lax.dot_general(
                right, left, (((1,), (1,)), ((), ())), preferred_element_type=f32
            )
        sums[...] = total

    gathered = sums[...].T
    s1 = gathered[:rx] + gathered[rx:2 * rx]
    s2 = gathered[2 * rx:3 * rx] + gathered[3 * rx:]

    @pl.when(gx == 0)
    def _():
        xin[...] = jnp.zeros_like(xin)

    @pl.when(gx == nx - 1)
    def _():
        xin_b[...] = jnp.zeros_like(xin_b)

    def rates_in_lanes(tile):
        wide = [jnp.zeros((8, LANES), f32)] * 2
        for v in range(variables):
            here = (lane >= v * rx) & (lane < (v + 1) * rx)
            wide = [jnp.where(here, new, old) for new, old in zip(rates(v, tile), wide)]
        return wide

    wait_row(edge, e_s, e_r)

    @pl.loop(0, tiles)
    def _(tile):
        rows = pl.ds(tile * 8, 8)
        sx, sy = rates_in_lanes(tile)
        total = jnp.zeros((8, LANES), f32)
        for src in range(ny):
            far = jnp.maximum(gy - 1 - src, 0).astype(f32) * ry
            total = total + jnp.where(src < gy, jnp.exp(-sy * far) * edge[src, rows, :], 0.0)
        inner = lax.rem(lane, rx)
        s = 1
        while s < rx:
            total = total + jnp.where(inner >= s, jnp.exp(-sx * s), 0.0) * pltpu.roll(total, s, 1)
            s *= 2
        q_ref[rows, :] = total * jnp.exp(-sy)

    for v in range(variables):
        @pl.when(gx > 0)
        def _():
            chain(v, xout, xin, x_s, x_r, gx).wait_recv()

        @pl.when(gx < nx - 1)
        def _():
            @pl.loop(0, tiles)
            def _(tile):
                rows = pl.ds(tile * 8, 8)
                sx, sy = rates(v, tile)
                spot = v * rx + rx - 1
                q = jnp.broadcast_to(q_ref[rows, spot:spot + 1], (8, LANES))
                mine = pl.ds(v * levels + tile * 8, 8)
                xout[v, rows, :] = (
                    field[rx - 1, mine, :] + fade[mine, :] * wide(q)
                    + wide(jnp.exp(-sx * rx)) * xin[v, rows, :]
                )
            chain(v, xout, xin, x_s, x_r, gx + 1).start()

        @pl.loop(0, tiles, unroll=2)
        def _(tile):
            rows = pl.ds(tile * 8, 8)
            mine = pl.ds(v * levels + tile * 8, 8)
            reach = fade[mine, :]
            q_all = q_ref[rows, :]
            ax = wide(axt[mine, :])
            entering = xin[v, rows, :]
            for x in range(rx):
                q = jnp.broadcast_to(q_all[:, v * rx + x:v * rx + x + 1], (8, LANES))
                entering = ax * entering
                field[x, mine, :] = field[x, mine, :] + reach * wide(q) + entering

    def soft_and_slope(value):
        small = jnp.exp(-jnp.abs(value))
        soft = jnp.maximum(value, 0.0) + jnp.log1p(small)
        return soft, jnp.where(value >= 0, 1.0, small) / (1.0 + small)

    @pl.loop(0, rx, unroll=4)
    def _(x):
        high, low = split(field[x])
        both = dot(mstack[...], high)
        value = both[:levels] + both[levels:] + dot(mstack[:levels, :], low) + base_levels[x]
        soft, slope = soft_and_slope(value)
        slopes[x] = slope
        totals[pl.ds(x, 1), :] = jnp.sum(wide(tab[3 * variables]) * soft, axis=0, keepdims=True)

    sp, sg = soft_and_slope(totals[...])
    sp_all[me] = sp
    totals[...] = sg * (sp * s1 - s2)
    start_all(sp_all, sp_s, sp_r)
    row0[...] = jnp.zeros_like(row0)

    @pl.loop(0, rx, unroll=4)
    def _(i):
        x = rx - 1 - i
        high, low = split(totals[pl.ds(x, 1), :] * slopes[x])
        back = dot(bstack[...], jnp.concatenate([high, low, high], axis=0))
        now = wide(axt[...]) * row0[...] + back
        row0[...] = now
        field[x] = now

    for v in range(variables):
        mine = slice(v * levels, (v + 1) * levels)

        @pl.loop(0, rx, unroll=4)
        def _(x):
            field[x, mine, :] = prefix(field[x, mine, :] * fade[mine, :], tri_b) * grow[mine, :]

        @pl.when(gx < nx - 1)
        def _():
            chain(v, xout_b, xin_b, b_s, b_r, gx).wait_recv()

        @pl.when(gx > 0)
        def _():
            xout_b[v] = row0[v * levels:(v + 1) * levels, :] + wide(
                jnp.exp(-tab[v] * rx)
            ) * xin_b[v]
            chain(v, xout_b, xin_b, b_s, b_r, gx - 1).start()

        row0[mine, :] = prefix(xin_b[v] * fade[mine, :], tri_b) * grow[mine, :]

        @pl.loop(0, tiles, unroll=2)
        def _(tile):
            rows = pl.ds(tile * 8, 8)
            here = pl.ds(v * levels + tile * 8, 8)
            ax = axt[here, :]
            first = jnp.broadcast_to(row0[here, :LANES][:, :1], (8, LANES))
            column = edge_b[gy, rows, :]
            for x in range(rx)[::-1]:
                own = field[x, here, :LANES][:, :1]
                first = ax * first
                column = jnp.where(
                    lane == v * rx + x, jnp.broadcast_to(own, (8, LANES)) + first, column
                )
            edge_b[gy, rows, :] = column

    start_row(edge_b, f_s, f_r)

    wait_all(sp_all, sp_s, sp_r)
    column_y = lax.broadcasted_iota(jnp.int32, (ry, count), 0).astype(f32)
    pick = jnp.where(column_y == cell_y, 1.0, 0.0).astype(bf16)
    batch = 8
    row_of = lax.broadcasted_iota(jnp.int32, (batch * rx, count), 0).astype(f32)

    def find(group, found):
        high, low = split(sp_all[pl.ds(group * batch, batch)].reshape(batch * rx, ry))
        value = dot(jnp.concatenate([high, low], axis=0), pick)
        value = value[:batch * rx] + value[batch * rx:]
        hit = row_of == key - (group * (batch * rx)).astype(f32)
        return found + jnp.sum(jnp.where(hit, value, 0.0).reshape(-1, 8, count), axis=0)

    found = lax.fori_loop(0, devices // batch, find, jnp.zeros((8, count), f32))
    found = jnp.sum(found, axis=0, keepdims=True)
    dep[...] = jnp.where(key >= 0, found - flash, 0.0)

    wait_row(edge_b, f_s, f_r)

    @pl.loop(0, tiles)
    def _(tile):
        rows = pl.ds(tile * 8, 8)
        sx, sy = rates_in_lanes(tile)
        total = jnp.zeros((8, LANES), f32)
        for src in range(ny):
            far = jnp.maximum(src - gy - 1, 0).astype(f32) * ry
            total = total + jnp.where(src > gy, jnp.exp(-sy * far) * edge_b[src, rows, :], 0.0)
        total = total * jnp.exp(-sy * ry)
        for v in range(variables):
            mine = pl.ds(v * levels + tile * 8, 8)
            reach = grow[mine, :]
            ax = wide(axt[mine, :])
            entering = row0[mine, :]
            for x in range(rx)[::-1]:
                q = jnp.broadcast_to(total[:, v * rx + x:v * rx + x + 1], (8, LANES))
                entering = ax * entering
                value = field[x, mine, :] + reach * wide(q) + entering
                for h in range(halves):
                    stage[v * halves + h, pl.ds(x, 8, stride=rx), :] = value[:, half(h)]
            for h in range(halves):
                at = (v, pl.ds(tile * 8 * rx, 8 * rx), half(h))
                out[at] = ctrl[at] + stage[v * halves + h]

    for v in range(variables):
        @pl.when(gx < nx - 1)
        def _():
            chain(v, xout, xin, x_s, x_r, gx + 1).wait_send()

        @pl.when(gx > 0)
        def _():
            chain(v, xout_b, xin_b, b_s, b_r, gx - 1).wait_send()


def body(
    control, background, vert_factor, length_rates, flash_weights, level_weights,
    obs_owner, obs_cell, obs_count, flash_obs, obs_error,
):
    variables, levels, rx, ry = control.shape
    nx, ny = lax.axis_size("gx"), lax.axis_size("gy")
    devices = nx * ny
    count = obs_cell.shape[0]
    vk = variables * levels
    step_x = length_rates[0] / (rx * nx)
    step_y = length_rates[1] / (ry * ny)
    gain = jnp.sqrt(jnp.expm1(-2.0 * step_x) * jnp.expm1(-2.0 * step_y))
    limit = jnp.broadcast_to(obs_count, (count,))
    seen = jnp.stack([
        obs_owner[:, 0].astype(f32), obs_cell.astype(f32), flash_obs, obs_error, limit.astype(f32)
    ])

    vmem = pl.BlockSpec(memory_space=pltpu.VMEM)
    dma = pltpu.SemaphoreType.DMA
    grad, departure = pl.pallas_call(
        functools.partial(kernel, nx, ny, variables, levels, rx, ry),
        out_shape=(
            jax.ShapeDtypeStruct((variables, levels * rx, ry), f32),
            jax.ShapeDtypeStruct((1, count), f32),
        ),
        in_specs=[vmem] * 8,
        out_specs=(vmem, vmem),
        scratch_shapes=[
            pltpu.VMEM((rx, vk, ry), f32),
            pltpu.VMEM((ry, 4 * rx), f32),
            pltpu.VMEM((devices, rx, ry), f32),
            pltpu.VMEM((devices, 8, count // 2), f32),
            pltpu.VMEM((ny, levels, LANES), f32),
            pltpu.VMEM((ny, levels, LANES), f32),
            pltpu.VMEM((levels, LANES), f32),
            pltpu.VMEM((variables, levels, ry), f32),
            pltpu.VMEM((variables, levels, ry), f32),
            pltpu.VMEM((variables, levels, ry), f32),
            pltpu.VMEM((variables, levels, ry), f32),
            pltpu.VMEM((vk, ry), f32),
            pltpu.VMEM((vk, LANES), f32),
            pltpu.VMEM((variables * ry // LANES, 8 * rx, LANES), f32),
            pltpu.VMEM((rx, levels, ry), f32),
            pltpu.VMEM((2 * levels, vk), bf16),
            pltpu.VMEM((vk, 3 * levels), bf16),
            pltpu.VMEM((3 * variables + 1, levels, LANES), f32),
            pltpu.VMEM((16, LANES), f32),
            pltpu.VMEM((ry, ry), bf16),
            pltpu.VMEM((ry, ry), bf16),
            pltpu.VMEM((vk, ry), f32),
            pltpu.VMEM((vk, ry), f32),
            pltpu.VMEM((rx, levels, ry), f32),
            pltpu.VMEM((rx, ry), f32),
            dma((devices,)), dma((devices,)), dma((devices,)), dma((devices,)),
            dma((ny,)), dma((ny,)), dma((ny,)), dma((ny,)),
            dma((variables,)), dma((variables,)), dma((variables,)), dma((variables,)),
        ],
        compiler_params=pltpu.CompilerParams(
            collective_id=0, has_side_effects=True, vmem_limit_bytes=48 * 2**20
        ),
    )(
        control.reshape(variables, levels * rx, ry),
        background.reshape(variables, levels * rx, ry),
        vert_factor, length_rates, gain, flash_weights, level_weights[None], seen,
    )
    return grad.reshape(control.shape), departure.reshape(count)


def solution(mesh):
    placed = (
        P(None, None, "gx", "gy"),
        P(None, None, "gx", "gy"),
        P(),
        P(),
        P(),
        P(),
        P(("gx", "gy"), None),
        P(("gx", "gy")),
        P(("gx", "gy")),
        P(("gx", "gy")),
        P(("gx", "gy")),
    )
    return jax.shard_map(
        body,
        mesh=mesh,
        in_specs=placed,
        out_specs=(P(None, None, "gx", "gy"), P(("gx", "gy"))),
        check_vma=False,
    )
```

```python
import functools
import jax
import jax.numpy as jnp
from jax import lax
from jax.experimental import pallas as pl
from jax.experimental.pallas import tpu as pltpu
from jax.sharding import PartitionSpec as P

LANES = 128
MESH = pl.DeviceIdType.MESH
f32, bf16 = jnp.float32, jnp.bfloat16


def split(value):
    high = value.astype(bf16)
    return high, (value - high.astype(f32)).astype(bf16)


def dot(left, right):
    return jnp.dot(left, right, preferred_element_type=f32)


def kernel(
    nx, ny, variables, levels, rx, ry,
    gain, ctrl_h, bg_h, vert_h, rate_h, flash_w_h, level_w_h, owner_h, cell_h, seen_h, error_h, live_h,
    out, dep,
    field, sums, sp_all, obs_all, edge, edge_b, q_ref, xin, xout, xin_b, xout_b, row0, axt, stage,
    base_levels, mstack, bstack, tab, raw, tri, tri_b, grow, fade, slopes, totals,
    qx, bx, ctrl, bg, vert, rate, flash_w, level_w, owner, cell, seen, error, live,
    in_s, ctrl_s, qx_s, qx_r, bx_s, bx_r,
    obs_s, obs_r, sp_s, sp_r, e_s, e_r, f_s, f_r, x_s, x_r, b_s, b_r,
):
    devices = nx * ny
    gx, gy = lax.axis_index("gx"), lax.axis_index("gy")
    me = gx * ny + gy
    halves = ry // LANES
    tiles = levels // 8
    vk = variables * levels
    lane = lax.broadcasted_iota(jnp.int32, (8, LANES), 1)
    small = [
        (vert_h, vert), (rate_h, rate), (flash_w_h, flash_w), (level_w_h, level_w),
        (owner_h, owner), (cell_h, cell), (seen_h, seen), (error_h, error), (live_h, live),
    ]
    small = [pltpu.make_async_copy(a, b, in_s.at[i + 1]) for i, (a, b) in enumerate(small)]
    bg_copy = pltpu.make_async_copy(bg_h, bg, in_s.at[0])
    ctrl_copy = [
        pltpu.make_async_copy(ctrl_h.at[v], ctrl.at[v], ctrl_s.at[v]) for v in range(variables)
    ]
    for copy in small + ctrl_copy + [bg_copy]:
        copy.start()

    def peer(offset):
        other = lax.rem(me + offset, devices)
        return (other // ny, lax.rem(other, ny))

    def to_all(ref, send, recv):
        def one(offset):
            return pltpu.make_async_remote_copy(
                ref.at[me], ref.at[me], send.at[offset], recv.at[me], peer(offset), MESH
            )
        return one

    def from_all(ref, send, recv, offset):
        src = lax.rem(me + offset, devices)
        return pltpu.make_async_remote_copy(
            ref.at[src], ref.at[src], send.at[offset], recv.at[src], peer(offset), MESH
        )

    def start_all(ref, send, recv):
        @pl.loop(1, devices)
        def _(offset):
            to_all(ref, send, recv)(offset).start()

    def wait_all(ref, send, recv):
        @pl.loop(1, devices)
        def _(offset):
            from_all(ref, send, recv, offset).wait_recv()
            to_all(ref, send, recv)(offset).wait_send()

    def row_copy(ref, send, recv, offset, slot):
        other = lax.rem(gy + offset, ny)
        return pltpu.make_async_remote_copy(
            ref.at[slot], ref.at[slot], send.at[offset], recv.at[slot], (gx, other), MESH
        )

    def start_row(ref, send, recv):
        @pl.loop(1, ny)
        def _(offset):
            row_copy(ref, send, recv, offset, gy).start()

    def wait_row(ref, send, recv):
        @pl.loop(1, ny)
        def _(offset):
            row_copy(ref, send, recv, offset, lax.rem(gy + offset, ny)).wait_recv()
            row_copy(ref, send, recv, offset, gy).wait_send()

    def chain(v, source, target, send, recv, other):
        return pltpu.make_async_remote_copy(
            source.at[v], target.at[v], send.at[v], recv.at[v], (other, gy), MESH
        )

    def half(h):
        return slice(h * LANES, (h + 1) * LANES)

    def rates(v, tile):
        rows = pl.ds(tile * 8, 8)
        return tab[v, rows, :], tab[variables + v, rows, :]

    barrier = pltpu.get_barrier_semaphore()

    @pl.loop(1, devices)
    def _(offset):
        pl.semaphore_signal(barrier, inc=1, device_id=peer(offset), device_id_type=MESH)
    for copy in small:
        copy.wait()
    pl.semaphore_wait(barrier, devices - 1)

    count = seen.shape[1]
    per = count // 2
    where = cell[...].astype(f32)
    cell_x = jnp.floor(where * (1.0 / ry))
    cell_y = where - cell_x * ry
    place = lax.broadcasted_iota(jnp.int32, (1, count), 1)
    key = jnp.where(place < live[...], owner[...].astype(f32) * rx + cell_x, -1.0)
    flash = seen[...]
    weight = 1.0 / (error[...] * error[...])
    for number, value in enumerate((key, cell_y, weight, flash * weight)):
        for part in range(2):
            obs_all[me, 2 * number + part:2 * number + part + 1, :] = value[
                :, part * per:(part + 1) * per
            ]
    start_all(obs_all, obs_s, obs_r)

    raw[...] = jnp.zeros_like(raw)
    raw[:variables, :levels] = rate[0] * (1.0 / (rx * nx))
    raw[variables:2 * variables, :levels] = rate[1] * (1.0 / (ry * ny))
    raw[2 * variables:3 * variables, :levels] = flash_w[...]
    raw[3 * variables:3 * variables + 1, :levels] = level_w[...]
    turned = raw[...].T
    for c in range(3 * variables + 1):
        tab[c] = jnp.broadcast_to(turned[:levels, c:c + 1], (levels, LANES))

    for v in range(variables):
        mine = slice(v * levels, (v + 1) * levels)
        scaled = vert[v] * gain[v:v + 1, :] * tab[2 * variables + v, :, :levels]
        high, low = split(scaled)
        mstack[:levels, mine] = high
        mstack[levels:, mine] = low
        high, low = split((scaled * tab[3 * variables, :, :levels]).T)
        bstack[mine, :levels] = high
        bstack[mine, levels:2 * levels] = high
        bstack[mine, 2 * levels:] = low
    down = lax.broadcasted_iota(jnp.int32, (ry, ry), 0)
    across = lax.broadcasted_iota(jnp.int32, (ry, ry), 1)
    tri[...] = jnp.where(down <= across, 1.0, 0.0).astype(bf16)
    tri_b[...] = jnp.where(down >= across, 1.0, 0.0).astype(bf16)

    def prefix(value, triangle):
        high, low = split(value)
        both = dot(jnp.concatenate([high, low], axis=0), triangle[...])
        return both[:value.shape[0]] + both[value.shape[0]:]

    wide = lambda value: jnp.concatenate([value] * halves, axis=1)
    position = lax.broadcasted_iota(jnp.int32, (8, ry), 1).astype(f32)

    edge[gy] = jnp.zeros((levels, LANES), f32)
    bx[gx] = jnp.zeros((levels, LANES), f32)

    @pl.when(gx == 0)
    def _():
        xin[...] = jnp.zeros_like(xin)

    @pl.when(gx == nx - 1)
    def _():
        xin_b[...] = jnp.zeros_like(xin_b)

    def step(slot, lag, last, next_x, own, source, target, send, recv):
        v = slot - lag

        @pl.when((v >= 0) & (v < variables))
        def _():
            @pl.when(lag > 0)
            def _():
                chain(v, source, target, send, recv, gx).wait_recv()

            @pl.when(lag < last)
            def _():
                source[v] = own(pl.ds(v * levels, levels)) + wide(
                    jnp.exp(-tab[v] * rx)
                ) * target[v]
                chain(v, source, target, send, recv, next_x).start()

    def step_forward(slot):
        step(slot, gx, nx - 1, gx + 1, lambda rows: field[rx - 1, rows, :], xout, xin, x_s, x_r)

    def step_back(slot):
        step(slot, nx - 1 - gx, nx - 1, gx - 1, lambda rows: row0[rows, :], xout_b, xin_b, b_s, b_r)

    slots = variables + nx - 1

    def corner(ref, send, recv, other, slot):
        return pltpu.make_async_remote_copy(
            ref.at[slot], ref.at[slot], send.at[other], recv.at[slot], (other, gy), MESH
        )

    def start_corner(ref, send, recv, ahead):
        for other in range(nx):
            @pl.when(ahead(gx, other))
            def _():
                corner(ref, send, recv, other, gx).start()

    def wait_corner(ref, send, recv, ahead):
        for other in range(nx):
            @pl.when(ahead(other, gx))
            def _():
                corner(ref, send, recv, other, other).wait_recv()

            @pl.when(ahead(gx, other))
            def _():
                corner(ref, send, recv, other, gx).wait_send()

    later, sooner = lambda a, b: b > a, lambda a, b: b < a
    inner = lax.rem(lane, rx)

    def scan_x(total, sx):
        s = 1
        while s < rx:
            total = total + jnp.where(inner >= s, jnp.exp(-sx * s), 0.0) * pltpu.roll(total, s, 1)
            s *= 2
        return total

    def rates_in_lanes(tile):
        both = [jnp.zeros((8, LANES), f32)] * 2
        for v in range(variables):
            here = (lane >= v * rx) & (lane < (v + 1) * rx)
            both = [jnp.where(here, new, old) for new, old in zip(rates(v, tile), both)]
        return both

    for v in range(variables):
        ctrl_copy[v].wait()

        @pl.loop(0, tiles // 2)
        def _(pair):
            parts, falls, decays = [], [], []
            for k in range(2):
                tile = pair * 2 + k
                rows = pl.ds(v * levels + tile * 8, 8)
                sx, sy = rates(v, tile)
                up, fall = jnp.exp(wide(sy) * position), jnp.exp(-wide(sy) * position)
                grow[rows, :], fade[rows, :] = up, fall
                ax = jnp.exp(-sx)
                axt[rows, :] = ax
                falls.append(fall)
                decays.append(wide(ax))
                for h in range(halves):
                    stage[k * halves + h] = ctrl[v, pl.ds(tile * 8 * rx, 8 * rx), half(h)]
                for x in range(rx):
                    strips = [
                        stage[k * halves + h, pl.ds(x, 8, stride=rx), :] for h in range(halves)
                    ]
                    parts.append(jnp.concatenate(strips, axis=1) * up)
            parts = prefix(jnp.concatenate(parts, axis=0), tri)
            for k in range(2):
                tile = pair * 2 + k
                rows = pl.ds(v * levels + tile * 8, 8)
                state = jnp.zeros((8, ry), f32)
                column = edge[gy, pl.ds(tile * 8, 8), :]
                for x in range(rx):
                    at = (k * rx + x) * 8
                    part = parts[at:at + 8] * falls[k]
                    last = jnp.broadcast_to(part[:, ry - 1:], (8, LANES))
                    column = jnp.where(lane == v * rx + x, last, column)
                    state = decays[k] * state + part
                    field[x, rows, :] = state
                edge[gy, pl.ds(tile * 8, 8), :] = column

        if v == variables - 1:
            start_row(edge, e_s, e_r)
        step_forward(v)

    bg_copy.wait()

    @pl.loop(0, tiles)
    def _(tile):
        for v in range(variables):
            for h in range(halves):
                stage[v * halves + h] = bg[v, pl.ds(tile * 8 * rx, 8 * rx), half(h)]
        weights = [tab[2 * variables + v, pl.ds(tile * 8, 8), :] for v in range(variables)]
        for x in range(rx):
            for h in range(halves):
                part = jnp.zeros((8, LANES), f32)
                for v in range(variables):
                    part = part + weights[v] * stage[v * halves + h, pl.ds(x, 8, stride=rx), :]
                base_levels[x, pl.ds(tile * 8, 8), half(h)] = part

    step_forward(variables)
    wait_all(obs_all, obs_s, obs_r)
    sums[...] = jnp.zeros_like(sums)
    row_x = lax.broadcasted_iota(jnp.int32, (rx, per), 0).astype(f32)
    row_y = lax.broadcasted_iota(jnp.int32, (ry, per), 0).astype(f32)
    base = (me * rx).astype(f32)

    @pl.loop(0, devices, unroll=2)
    def _(src):
        pieces, rights = [], []
        for part in range(2):
            hit = row_x == obs_all[src, part:part + 1, :] - base
            spot = obs_all[src, 2 + part:3 + part, :]
            rows = []
            for field_of in (4, 6):
                load = obs_all[src, field_of + part:field_of + part + 1, :]
                rows += split(jnp.where(hit, load, 0.0))
            pieces.append(jnp.concatenate(rows, axis=0))
            rights.append(jnp.where(row_y == spot, 1.0, 0.0).astype(bf16))
        sums[...] += lax.dot_general(
            jnp.concatenate(rights, axis=1), jnp.concatenate(pieces, axis=1),
            (((1,), (1,)), ((), ())), preferred_element_type=f32,
        )

    gathered = sums[...].T
    s1 = gathered[:rx] + gathered[rx:2 * rx]
    s2 = gathered[2 * rx:3 * rx] + gathered[3 * rx:]

    step_forward(variables + 1)
    wait_row(edge, e_s, e_r)

    @pl.loop(0, tiles)
    def _(tile):
        rows = pl.ds(tile * 8, 8)
        sx, sy = rates_in_lanes(tile)
        total = jnp.zeros((8, LANES), f32)
        for src in range(ny):
            far = jnp.maximum(gy - 1 - src, 0).astype(f32) * ry
            total = total + jnp.where(src < gy, jnp.exp(-sy * far) * edge[src, rows, :], 0.0)
        q_ref[rows, :] = total
        qx[gx, rows, :] = scan_x(total, sx)

    start_corner(qx, qx_s, qx_r, later)
    for slot in range(variables + 2, slots):
        step_forward(slot)
    wait_corner(qx, qx_s, qx_r, later)

    @pl.loop(0, tiles)
    def _(tile):
        rows = pl.ds(tile * 8, 8)
        sx, sy = rates_in_lanes(tile)
        total = jnp.zeros((8, LANES), f32)
        for src in range(nx):
            far = jnp.maximum(gx - 1 - src, 0).astype(f32) * rx
            total = total + jnp.where(src < gx, jnp.exp(-sx * far) * qx[src, rows, :], 0.0)
        total = jnp.exp(-sx) * pltpu.roll(total, LANES - (rx - 1), 1)
        total = q_ref[rows, :] + jnp.where(inner == 0, total, 0.0)
        q_ref[rows, :] = scan_x(total, sx) * jnp.exp(-sy)

    for v in range(variables):
        @pl.loop(0, tiles, unroll=2)
        def _(tile):
            rows = pl.ds(tile * 8, 8)
            mine = pl.ds(v * levels + tile * 8, 8)
            reach = fade[mine, :]
            q_all = q_ref[rows, :]
            ax = wide(axt[mine, :])
            entering = xin[v, rows, :]
            for x in range(rx):
                q = jnp.broadcast_to(q_all[:, v * rx + x:v * rx + x + 1], (8, LANES))
                entering = ax * entering
                field[x, mine, :] = field[x, mine, :] + reach * wide(q) + entering

    def soft_and_slope(value):
        small = jnp.exp(-jnp.abs(value))
        soft = jnp.maximum(value, 0.0) + jnp.log1p(small)
        return soft, jnp.where(value >= 0, 1.0, small) / (1.0 + small)

    @pl.loop(0, rx, unroll=4)
    def _(x):
        high, low = split(field[x])
        both = dot(mstack[...], high)
        value = both[:levels] + both[levels:] + dot(mstack[:levels, :], low) + base_levels[x]
        soft, slope = soft_and_slope(value)
        slopes[x] = slope
        totals[pl.ds(x, 1), :] = jnp.sum(wide(tab[3 * variables]) * soft, axis=0, keepdims=True)

    sp, sg = soft_and_slope(totals[...])
    sp_all[me] = sp
    totals[...] = sg * (sp * s1 - s2)
    start_all(sp_all, sp_s, sp_r)
    row0[...] = jnp.zeros_like(row0)

    @pl.loop(0, rx, unroll=4)
    def _(i):
        x = rx - 1 - i
        high, low = split(totals[pl.ds(x, 1), :] * slopes[x])
        back = dot(bstack[...], jnp.concatenate([high, low, high], axis=0))
        now = wide(axt[...]) * row0[...] + back
        row0[...] = now
        field[x] = now

    for v in range(variables):
        mine = slice(v * levels, (v + 1) * levels)

        @pl.loop(0, rx // 4)
        def _(group):
            lag, lead = fade[mine, :][None], grow[mine, :][None]
            value = field[pl.ds(group * 4, 4), mine, :] * lag
            value = prefix(value.reshape(4 * levels, ry), tri_b).reshape(4, levels, ry)
            field[pl.ds(group * 4, 4), mine, :] = value * lead

        @pl.loop(0, tiles, unroll=2)
        def _(tile):
            rows = pl.ds(tile * 8, 8)
            here = pl.ds(v * levels + tile * 8, 8)
            column = bx[gx, rows, :]
            for x in range(rx):
                own = field[x, here, :LANES][:, :1]
                column = jnp.where(lane == v * rx + x, jnp.broadcast_to(own, (8, LANES)), column)
            bx[gx, rows, :] = column

        if v == variables - 1:
            start_corner(bx, bx_s, bx_r, sooner)
        step_back(v)

    wait_corner(bx, bx_s, bx_r, sooner)

    @pl.loop(0, tiles)
    def _(tile):
        rows = pl.ds(tile * 8, 8)
        sx, sy = rates_in_lanes(tile)
        total = jnp.zeros((8, LANES), f32)
        for src in range(nx):
            far = jnp.maximum(src - gx - 1, 0).astype(f32) * rx
            total = total + jnp.where(src > gx, jnp.exp(-sx * far) * bx[src, rows, :], 0.0)
        total = jnp.where(inner == 0, total, 0.0)
        s = 1
        while s < rx:
            total = total + jnp.where((inner >= s) & (inner < 2 * s), pltpu.roll(total, s, 1), 0.0)
            s *= 2
        edge_b[gy, rows, :] = bx[gx, rows, :] + jnp.exp(-sx * (rx - inner).astype(f32)) * total

    start_row(edge_b, f_s, f_r)
    step_back(variables)
    wait_all(sp_all, sp_s, sp_r)
    column_y = lax.broadcasted_iota(jnp.int32, (ry, count), 0).astype(f32)
    pick = jnp.where(column_y == cell_y, 1.0, 0.0).astype(bf16)
    batch = 8
    row_of = lax.broadcasted_iota(jnp.int32, (batch * rx, count), 0).astype(f32)

    def find(group, found):
        high, low = split(sp_all[pl.ds(group * batch, batch)].reshape(batch * rx, ry))
        value = dot(jnp.concatenate([high, low], axis=0), pick)
        value = value[:batch * rx] + value[batch * rx:]
        hit = row_of == key - (group * (batch * rx)).astype(f32)
        return found + jnp.sum(jnp.where(hit, value, 0.0).reshape(-1, 8, count), axis=0)

    found = lax.fori_loop(0, devices // batch, find, jnp.zeros((8, count), f32))
    found = jnp.sum(found, axis=0, keepdims=True)
    dep[...] = jnp.where(key >= 0, found - flash, 0.0)

    for slot in range(variables + 1, slots):
        step_back(slot)
    entered = xin_b[...].reshape(vk, ry) * fade[...]
    row0[...] = prefix(entered, tri_b) * grow[...]
    wait_row(edge_b, f_s, f_r)

    @pl.loop(0, tiles)
    def _(tile):
        rows = pl.ds(tile * 8, 8)
        sx, sy = rates_in_lanes(tile)
        total = jnp.zeros((8, LANES), f32)
        for src in range(ny):
            far = jnp.maximum(src - gy - 1, 0).astype(f32) * ry
            total = total + jnp.where(src > gy, jnp.exp(-sy * far) * edge_b[src, rows, :], 0.0)
        total = total * jnp.exp(-sy * ry)
        for v in range(variables):
            mine = pl.ds(v * levels + tile * 8, 8)
            reach = grow[mine, :]
            ax = wide(axt[mine, :])
            entering = row0[mine, :]
            for x in range(rx)[::-1]:
                q = jnp.broadcast_to(total[:, v * rx + x:v * rx + x + 1], (8, LANES))
                entering = ax * entering
                value = field[x, mine, :] + reach * wide(q) + entering
                for h in range(halves):
                    stage[v * halves + h, pl.ds(x, 8, stride=rx), :] = value[:, half(h)]
            for h in range(halves):
                at = (v, pl.ds(tile * 8 * rx, 8 * rx), half(h))
                out[at] = ctrl[at] + stage[v * halves + h]

    for v in range(variables):
        @pl.when(gx < nx - 1)
        def _():
            chain(v, xout, xin, x_s, x_r, gx + 1).wait_send()

        @pl.when(gx > 0)
        def _():
            chain(v, xout_b, xin_b, b_s, b_r, gx - 1).wait_send()


def body(
    control, background, vert_factor, length_rates, flash_weights, level_weights,
    obs_owner, obs_cell, obs_count, flash_obs, obs_error,
):
    variables, levels, rx, ry = control.shape
    nx, ny = lax.axis_size("gx"), lax.axis_size("gy")
    devices = nx * ny
    count = obs_cell.shape[0]
    vk = variables * levels
    step_x = length_rates[0] / (rx * nx)
    step_y = length_rates[1] / (ry * ny)
    gain = jnp.sqrt(jnp.expm1(-2.0 * step_x) * jnp.expm1(-2.0 * step_y))
    vmem = pl.BlockSpec(memory_space=pltpu.VMEM)
    dma = pltpu.SemaphoreType.DMA
    grad, departure = pl.pallas_call(
        functools.partial(kernel, nx, ny, variables, levels, rx, ry),
        out_shape=(
            jax.ShapeDtypeStruct((variables, levels * rx, ry), f32),
            jax.ShapeDtypeStruct((1, count), f32),
        ),
        in_specs=[vmem] + [pl.BlockSpec(memory_space=pltpu.HBM)] * 11,
        out_specs=(vmem, vmem),
        scratch_shapes=[
            pltpu.VMEM((rx, vk, ry), f32),
            pltpu.VMEM((ry, 4 * rx), f32),
            pltpu.VMEM((devices, rx, ry), f32),
            pltpu.VMEM((devices, 8, count // 2), f32),
            pltpu.VMEM((ny, levels, LANES), f32),
            pltpu.VMEM((ny, levels, LANES), f32),
            pltpu.VMEM((levels, LANES), f32),
            pltpu.VMEM((variables, levels, ry), f32),
            pltpu.VMEM((variables, levels, ry), f32),
            pltpu.VMEM((variables, levels, ry), f32),
            pltpu.VMEM((variables, levels, ry), f32),
            pltpu.VMEM((vk, ry), f32),
            pltpu.VMEM((vk, LANES), f32),
            pltpu.VMEM((variables * ry // LANES, 8 * rx, LANES), f32),
            pltpu.VMEM((rx, levels, ry), f32),
            pltpu.VMEM((2 * levels, vk), bf16),
            pltpu.VMEM((vk, 3 * levels), bf16),
            pltpu.VMEM((3 * variables + 1, levels, LANES), f32),
            pltpu.VMEM((16, LANES), f32),
            pltpu.VMEM((ry, ry), bf16),
            pltpu.VMEM((ry, ry), bf16),
            pltpu.VMEM((vk, ry), f32),
            pltpu.VMEM((vk, ry), f32),
            pltpu.VMEM((rx, levels, ry), f32),
            pltpu.VMEM((rx, ry), f32),
            pltpu.VMEM((nx, levels, LANES), f32),
            pltpu.VMEM((nx, levels, LANES), f32),
            pltpu.VMEM((variables, levels * rx, ry), f32),
            pltpu.VMEM((variables, levels * rx, ry), f32),
            pltpu.VMEM((variables, levels, levels), f32),
            pltpu.VMEM((2, variables, levels), f32),
            pltpu.VMEM((variables, levels), f32),
            pltpu.VMEM((1, levels), f32),
            pltpu.VMEM((1, count), jnp.int32),
            pltpu.VMEM((1, count), jnp.int32),
            pltpu.VMEM((1, count), f32),
            pltpu.VMEM((1, count), f32),
            pltpu.VMEM((1, 1), jnp.int32),
            dma((10,)), dma((variables,)), dma((nx,)), dma((nx,)), dma((nx,)), dma((nx,)),
            dma((devices,)), dma((devices,)), dma((devices,)), dma((devices,)),
            dma((ny,)), dma((ny,)), dma((ny,)), dma((ny,)),
            dma((variables,)), dma((variables,)), dma((variables,)), dma((variables,)),
        ],
        compiler_params=pltpu.CompilerParams(
            collective_id=0, has_side_effects=True, vmem_limit_bytes=58 * 2**20
        ),
    )(
        gain, control.reshape(variables, levels * rx, ry),
        background.reshape(variables, levels * rx, ry),
        vert_factor, length_rates, flash_weights, level_weights[None], obs_owner.reshape(1, count),
        obs_cell[None], flash_obs[None], obs_error[None], obs_count[None],
    )
    return grad.reshape(control.shape), departure.reshape(count)


def solution(mesh):
    placed = (
        P(None, None, "gx", "gy"),
        P(None, None, "gx", "gy"),
        P(),
        P(),
        P(),
        P(),
        P(("gx", "gy"), None),
        P(("gx", "gy")),
        P(("gx", "gy")),
        P(("gx", "gy")),
        P(("gx", "gy")),
    )
    return jax.shard_map(
        body,
        mesh=mesh,
        in_specs=placed,
        out_specs=(P(None, None, "gx", "gy"), P(("gx", "gy"))),
        check_vma=False,
    )
```

```python
import functools
import jax
import jax.numpy as jnp
from jax import lax
from jax.experimental import pallas as pl
from jax.experimental.pallas import tpu as pltpu
from jax.sharding import PartitionSpec as P

LANES = 128
MESH = pl.DeviceIdType.MESH
f32, bf16 = jnp.float32, jnp.bfloat16


def split(value):
    high = value.astype(bf16)
    return high, (value - high.astype(f32)).astype(bf16)


def dot(left, right):
    return jnp.dot(left, right, preferred_element_type=f32)


def kernel(
    nx, ny, variables, levels, rx, ry,
    gain, ctrl_h, bg_h, vert_h, rate_h, flash_w_h, level_w_h, owner_h, cell_h, seen_h, error_h, live_h,
    field, row0, grow, axt, ending, dep,
    sums, sp_all, obs_all, edge, edge_b, q_ref, xin, xout, xin_b, xout_b, stage,
    base_levels, mstack, bstack, tab, raw, tri, tri_b, fade, slopes, totals,
    qx, bx, ctrl, bg, vert, rate, flash_w, level_w, owner, cell, seen, error, live,
    in_s, ctrl_s, qx_s, qx_r, bx_s, bx_r,
    obs_s, obs_r, sp_s, sp_r, e_s, e_r, f_s, f_r, x_s, x_r, b_s, b_r,
):
    devices = nx * ny
    gx, gy = lax.axis_index("gx"), lax.axis_index("gy")
    me = gx * ny + gy
    halves = ry // LANES
    tiles = levels // 8
    vk = variables * levels
    lane = lax.broadcasted_iota(jnp.int32, (8, LANES), 1)
    small = [
        (vert_h, vert), (rate_h, rate), (flash_w_h, flash_w), (level_w_h, level_w),
        (owner_h, owner), (cell_h, cell), (seen_h, seen), (error_h, error), (live_h, live),
    ]
    small = [pltpu.make_async_copy(a, b, in_s.at[i + 1]) for i, (a, b) in enumerate(small)]
    bg_copy = pltpu.make_async_copy(bg_h, bg, in_s.at[0])
    ctrl_copy = [
        pltpu.make_async_copy(ctrl_h.at[v], ctrl.at[v], ctrl_s.at[v]) for v in range(variables)
    ]
    for copy in small + ctrl_copy + [bg_copy]:
        copy.start()

    def peer(offset):
        other = lax.rem(me + offset, devices)
        return (other // ny, lax.rem(other, ny))

    def to_all(ref, send, recv):
        def one(offset):
            return pltpu.make_async_remote_copy(
                ref.at[me], ref.at[me], send.at[offset], recv.at[me], peer(offset), MESH
            )
        return one

    def from_all(ref, send, recv, offset):
        src = lax.rem(me + offset, devices)
        return pltpu.make_async_remote_copy(
            ref.at[src], ref.at[src], send.at[offset], recv.at[src], peer(offset), MESH
        )

    def start_all(ref, send, recv):
        @pl.loop(1, devices)
        def _(offset):
            to_all(ref, send, recv)(offset).start()

    def wait_all(ref, send, recv):
        @pl.loop(1, devices)
        def _(offset):
            from_all(ref, send, recv, offset).wait_recv()
            to_all(ref, send, recv)(offset).wait_send()

    def row_copy(ref, send, recv, offset, slot):
        other = lax.rem(gy + offset, ny)
        return pltpu.make_async_remote_copy(
            ref.at[slot], ref.at[slot], send.at[offset], recv.at[slot], (gx, other), MESH
        )

    def start_row(ref, send, recv):
        @pl.loop(1, ny)
        def _(offset):
            row_copy(ref, send, recv, offset, gy).start()

    def wait_row(ref, send, recv):
        @pl.loop(1, ny)
        def _(offset):
            row_copy(ref, send, recv, offset, lax.rem(gy + offset, ny)).wait_recv()
            row_copy(ref, send, recv, offset, gy).wait_send()

    def chain(v, source, target, send, recv, other):
        return pltpu.make_async_remote_copy(
            source.at[v], target.at[v], send.at[v], recv.at[v], (other, gy), MESH
        )

    def half(h):
        return slice(h * LANES, (h + 1) * LANES)

    def rates(v, tile):
        rows = pl.ds(tile * 8, 8)
        return tab[v, rows, :], tab[variables + v, rows, :]

    barrier = pltpu.get_barrier_semaphore()

    @pl.loop(1, devices)
    def _(offset):
        pl.semaphore_signal(barrier, inc=1, device_id=peer(offset), device_id_type=MESH)
    for copy in small:
        copy.wait()

    count = seen.shape[1]
    per = count // 2
    where = cell[...].astype(f32)
    cell_x = jnp.floor(where * (1.0 / ry))
    cell_y = where - cell_x * ry
    place = lax.broadcasted_iota(jnp.int32, (1, count), 1)
    key = jnp.where(place < live[...], owner[...].astype(f32) * rx + cell_x, -1.0)
    flash = seen[...]
    weight = 1.0 / (error[...] * error[...])
    for number, value in enumerate((key, cell_y, weight, flash * weight)):
        for part in range(2):
            obs_all[me, 2 * number + part:2 * number + part + 1, :] = value[
                :, part * per:(part + 1) * per
            ]

    raw[...] = jnp.zeros_like(raw)
    raw[:variables, :levels] = rate[0] * (1.0 / (rx * nx))
    raw[variables:2 * variables, :levels] = rate[1] * (1.0 / (ry * ny))
    raw[2 * variables:3 * variables, :levels] = flash_w[...]
    raw[3 * variables:3 * variables + 1, :levels] = level_w[...]
    turned = raw[...].T
    for c in range(3 * variables + 1):
        tab[c] = jnp.broadcast_to(turned[:levels, c:c + 1], (levels, LANES))

    for v in range(variables):
        mine = slice(v * levels, (v + 1) * levels)
        scaled = vert[v] * gain[v:v + 1, :] * tab[2 * variables + v, :, :levels]
        high, low = split(scaled)
        mstack[:levels, mine] = high
        mstack[levels:, mine] = low
        high, low = split((scaled * tab[3 * variables, :, :levels]).T)
        bstack[mine, :levels] = high
        bstack[mine, levels:2 * levels] = high
        bstack[mine, 2 * levels:] = low
    down = lax.broadcasted_iota(jnp.int32, (ry, ry), 0)
    across = lax.broadcasted_iota(jnp.int32, (ry, ry), 1)
    tri[...] = jnp.where(down <= across, 1.0, 0.0).astype(bf16)
    tri_b[...] = jnp.where(down >= across, 1.0, 0.0).astype(bf16)

    def prefix(value, triangle):
        high, low = split(value)
        both = dot(jnp.concatenate([high, low], axis=0), triangle[...])
        return both[:value.shape[0]] + both[value.shape[0]:]

    wide = lambda value: jnp.concatenate([value] * halves, axis=1)
    position = lax.broadcasted_iota(jnp.int32, (8, ry), 1).astype(f32)

    edge[gy] = jnp.zeros((levels, LANES), f32)
    bx[gx] = jnp.zeros((levels, LANES), f32)

    @pl.when(gx == 0)
    def _():
        xin[...] = jnp.zeros_like(xin)

    @pl.when(gx == nx - 1)
    def _():
        xin_b[...] = jnp.zeros_like(xin_b)

    def step(slot, lag, last, next_x, own, source, target, send, recv):
        v = slot - lag

        @pl.when((v >= 0) & (v < variables))
        def _():
            @pl.when(lag > 0)
            def _():
                chain(v, source, target, send, recv, gx).wait_recv()

            @pl.when(lag < last)
            def _():
                source[v] = own(pl.ds(v * levels, levels)) + wide(
                    jnp.exp(-tab[v] * rx)
                ) * target[v]
                chain(v, source, target, send, recv, next_x).start()

    def step_forward(slot):
        step(slot, gx, nx - 1, gx + 1, lambda rows: field[rx - 1, rows, :], xout, xin, x_s, x_r)

    def step_back(slot):
        step(slot, nx - 1 - gx, nx - 1, gx - 1, lambda rows: row0[rows, :], xout_b, xin_b, b_s, b_r)

    slots = variables + nx - 1

    def corner(ref, send, recv, other, slot):
        return pltpu.make_async_remote_copy(
            ref.at[slot], ref.at[slot], send.at[other], recv.at[slot], (other, gy), MESH
        )

    def start_corner(ref, send, recv, ahead):
        for other in range(nx):
            @pl.when(ahead(gx, other))
            def _():
                corner(ref, send, recv, other, gx).start()

    def wait_corner(ref, send, recv, ahead):
        for other in range(nx):
            @pl.when(ahead(other, gx))
            def _():
                corner(ref, send, recv, other, other).wait_recv()

            @pl.when(ahead(gx, other))
            def _():
                corner(ref, send, recv, other, gx).wait_send()

    later, sooner = lambda a, b: b > a, lambda a, b: b < a
    inner = lax.rem(lane, rx)

    def scan_x(total, sx):
        s = 1
        while s < rx:
            total = total + jnp.where(inner >= s, jnp.exp(-sx * s), 0.0) * pltpu.roll(total, s, 1)
            s *= 2
        return total

    def rates_in_lanes(tile):
        both = [jnp.zeros((8, LANES), f32)] * 2
        for v in range(variables):
            here = (lane >= v * rx) & (lane < (v + 1) * rx)
            both = [jnp.where(here, new, old) for new, old in zip(rates(v, tile), both)]
        return both

    for v in range(variables):
        ctrl_copy[v].wait()

        @pl.loop(0, tiles // 2)
        def _(pair):
            parts, falls, decays = [], [], []
            for k in range(2):
                tile = pair * 2 + k
                rows = pl.ds(v * levels + tile * 8, 8)
                sx, sy = rates(v, tile)
                up, fall = jnp.exp(wide(sy) * position), jnp.exp(-wide(sy) * position)
                grow[rows, :], fade[rows, :] = up, fall
                ax = jnp.exp(-sx)
                axt[rows, :] = ax
                falls.append(fall)
                decays.append(wide(ax))
                for h in range(halves):
                    stage[k * halves + h] = ctrl[v, pl.ds(tile * 8 * rx, 8 * rx), half(h)]
                for x in range(rx):
                    strips = [
                        stage[k * halves + h, pl.ds(x, 8, stride=rx), :] for h in range(halves)
                    ]
                    parts.append(jnp.concatenate(strips, axis=1) * up)
            parts = prefix(jnp.concatenate(parts, axis=0), tri)
            for k in range(2):
                tile = pair * 2 + k
                rows = pl.ds(v * levels + tile * 8, 8)
                state = jnp.zeros((8, ry), f32)
                column = edge[gy, pl.ds(tile * 8, 8), :]
                for x in range(rx):
                    at = (k * rx + x) * 8
                    part = parts[at:at + 8] * falls[k]
                    last = jnp.broadcast_to(part[:, ry - 1:], (8, LANES))
                    column = jnp.where(lane == v * rx + x, last, column)
                    state = decays[k] * state + part
                    field[x, rows, :] = state
                edge[gy, pl.ds(tile * 8, 8), :] = column

        if v == 0:
            pl.semaphore_wait(barrier, devices - 1)
            start_all(obs_all, obs_s, obs_r)
        if v == variables - 1:
            start_row(edge, e_s, e_r)
        step_forward(v)

    bg_copy.wait()

    @pl.loop(0, tiles)
    def _(tile):
        for v in range(variables):
            for h in range(halves):
                stage[v * halves + h] = bg[v, pl.ds(tile * 8 * rx, 8 * rx), half(h)]
        weights = [tab[2 * variables + v, pl.ds(tile * 8, 8), :] for v in range(variables)]
        for x in range(rx):
            for h in range(halves):
                part = jnp.zeros((8, LANES), f32)
                for v in range(variables):
                    part = part + weights[v] * stage[v * halves + h, pl.ds(x, 8, stride=rx), :]
                base_levels[x, pl.ds(tile * 8, 8), half(h)] = part

    step_forward(variables)
    wait_all(obs_all, obs_s, obs_r)
    sums[...] = jnp.zeros_like(sums)
    row_x = lax.broadcasted_iota(jnp.int32, (rx, per), 0).astype(f32)
    row_y = lax.broadcasted_iota(jnp.int32, (ry, per), 0).astype(f32)
    base = (me * rx).astype(f32)

    @pl.loop(0, devices, unroll=2)
    def _(src):
        pieces, rights = [], []
        for part in range(2):
            hit = row_x == obs_all[src, part:part + 1, :] - base
            spot = obs_all[src, 2 + part:3 + part, :]
            rows = []
            for field_of in (4, 6):
                load = obs_all[src, field_of + part:field_of + part + 1, :]
                rows += split(jnp.where(hit, load, 0.0))
            pieces.append(jnp.concatenate(rows, axis=0))
            rights.append(jnp.where(row_y == spot, 1.0, 0.0).astype(bf16))
        sums[...] += lax.dot_general(
            jnp.concatenate(rights, axis=1), jnp.concatenate(pieces, axis=1),
            (((1,), (1,)), ((), ())), preferred_element_type=f32,
        )

    gathered = sums[...].T
    s1 = gathered[:rx] + gathered[rx:2 * rx]
    s2 = gathered[2 * rx:3 * rx] + gathered[3 * rx:]

    step_forward(variables + 1)
    wait_row(edge, e_s, e_r)

    @pl.loop(0, tiles)
    def _(tile):
        rows = pl.ds(tile * 8, 8)
        sx, sy = rates_in_lanes(tile)
        total = jnp.zeros((8, LANES), f32)
        for src in range(ny):
            far = jnp.maximum(gy - 1 - src, 0).astype(f32) * ry
            total = total + jnp.where(src < gy, jnp.exp(-sy * far) * edge[src, rows, :], 0.0)
        q_ref[rows, :] = total
        qx[gx, rows, :] = scan_x(total, sx)

    start_corner(qx, qx_s, qx_r, later)
    for slot in range(variables + 2, slots):
        step_forward(slot)
    wait_corner(qx, qx_s, qx_r, later)

    @pl.loop(0, tiles)
    def _(tile):
        rows = pl.ds(tile * 8, 8)
        sx, sy = rates_in_lanes(tile)
        total = jnp.zeros((8, LANES), f32)
        for src in range(nx):
            far = jnp.maximum(gx - 1 - src, 0).astype(f32) * rx
            total = total + jnp.where(src < gx, jnp.exp(-sx * far) * qx[src, rows, :], 0.0)
        total = jnp.exp(-sx) * pltpu.roll(total, LANES - (rx - 1), 1)
        total = q_ref[rows, :] + jnp.where(inner == 0, total, 0.0)
        q_ref[rows, :] = scan_x(total, sx) * jnp.exp(-sy)

    for v in range(variables):
        @pl.loop(0, tiles, unroll=2)
        def _(tile):
            rows = pl.ds(tile * 8, 8)
            mine = pl.ds(v * levels + tile * 8, 8)
            reach = fade[mine, :]
            q_all = q_ref[rows, :]
            ax = wide(axt[mine, :])
            entering = xin[v, rows, :]
            for x in range(rx):
                q = jnp.broadcast_to(q_all[:, v * rx + x:v * rx + x + 1], (8, LANES))
                entering = ax * entering
                field[x, mine, :] = field[x, mine, :] + reach * wide(q) + entering

    def soft_and_slope(value):
        small = jnp.exp(-jnp.abs(value))
        soft = jnp.maximum(value, 0.0) + jnp.log1p(small)
        return soft, jnp.where(value >= 0, 1.0, small) / (1.0 + small)

    @pl.loop(0, rx, unroll=4)
    def _(x):
        high, low = split(field[x])
        both = dot(mstack[...], high)
        value = both[:levels] + both[levels:] + dot(mstack[:levels, :], low) + base_levels[x]
        soft, slope = soft_and_slope(value)
        slopes[x] = slope
        totals[pl.ds(x, 1), :] = jnp.sum(wide(tab[3 * variables]) * soft, axis=0, keepdims=True)

    sp, sg = soft_and_slope(totals[...])
    sp_all[me] = sp
    totals[...] = sg * (sp * s1 - s2)
    start_all(sp_all, sp_s, sp_r)
    row0[...] = jnp.zeros_like(row0)

    @pl.loop(0, rx, unroll=4)
    def _(i):
        x = rx - 1 - i
        high, low = split(totals[pl.ds(x, 1), :] * slopes[x])
        back = dot(bstack[...], jnp.concatenate([high, low, high], axis=0))
        now = wide(axt[...]) * row0[...] + back
        row0[...] = now
        field[x] = now

    for v in range(variables):
        mine = slice(v * levels, (v + 1) * levels)

        @pl.loop(0, rx // 4)
        def _(group):
            lag, lead = fade[mine, :][None], grow[mine, :][None]
            value = field[pl.ds(group * 4, 4), mine, :] * lag
            value = prefix(value.reshape(4 * levels, ry), tri_b).reshape(4, levels, ry)
            field[pl.ds(group * 4, 4), mine, :] = value * lead

        @pl.loop(0, tiles, unroll=2)
        def _(tile):
            rows = pl.ds(tile * 8, 8)
            here = pl.ds(v * levels + tile * 8, 8)
            column = bx[gx, rows, :]
            for x in range(rx):
                own = field[x, here, :LANES][:, :1]
                column = jnp.where(lane == v * rx + x, jnp.broadcast_to(own, (8, LANES)), column)
            bx[gx, rows, :] = column

        if v == variables - 1:
            start_corner(bx, bx_s, bx_r, sooner)
        step_back(v)

    wait_corner(bx, bx_s, bx_r, sooner)

    @pl.loop(0, tiles)
    def _(tile):
        rows = pl.ds(tile * 8, 8)
        sx, sy = rates_in_lanes(tile)
        total = jnp.zeros((8, LANES), f32)
        for src in range(nx):
            far = jnp.maximum(src - gx - 1, 0).astype(f32) * rx
            total = total + jnp.where(src > gx, jnp.exp(-sx * far) * bx[src, rows, :], 0.0)
        total = jnp.where(inner == 0, total, 0.0)
        s = 1
        while s < rx:
            total = total + jnp.where((inner >= s) & (inner < 2 * s), pltpu.roll(total, s, 1), 0.0)
            s *= 2
        edge_b[gy, rows, :] = bx[gx, rows, :] + jnp.exp(-sx * (rx - inner).astype(f32)) * total

    start_row(edge_b, f_s, f_r)
    step_back(variables)
    wait_all(sp_all, sp_s, sp_r)
    column_y = lax.broadcasted_iota(jnp.int32, (ry, count), 0).astype(f32)
    pick = jnp.where(column_y == cell_y, 1.0, 0.0).astype(bf16)
    batch = 8
    row_of = lax.broadcasted_iota(jnp.int32, (batch * rx, count), 0).astype(f32)

    def find(group, found):
        high, low = split(sp_all[pl.ds(group * batch, batch)].reshape(batch * rx, ry))
        value = dot(jnp.concatenate([high, low], axis=0), pick)
        value = value[:batch * rx] + value[batch * rx:]
        hit = row_of == key - (group * (batch * rx)).astype(f32)
        return found + jnp.sum(jnp.where(hit, value, 0.0).reshape(-1, 8, count), axis=0)

    found = lax.fori_loop(0, devices // batch, find, jnp.zeros((8, count), f32))
    found = jnp.sum(found, axis=0, keepdims=True)
    dep[...] = jnp.where(key >= 0, found - flash, 0.0)

    for slot in range(variables + 1, slots):
        step_back(slot)
    entered = xin_b[...].reshape(vk, ry) * fade[...]
    row0[...] = prefix(entered, tri_b) * grow[...]
    wait_row(edge_b, f_s, f_r)

    @pl.loop(0, tiles)
    def _(tile):
        rows = pl.ds(tile * 8, 8)
        sx, sy = rates_in_lanes(tile)
        total = jnp.zeros((8, LANES), f32)
        for src in range(ny):
            far = jnp.maximum(src - gy - 1, 0).astype(f32) * ry
            total = total + jnp.where(src > gy, jnp.exp(-sy * far) * edge_b[src, rows, :], 0.0)
        ending[rows, :] = total * jnp.exp(-sy * ry)

    for v in range(variables):
        @pl.when(gx < nx - 1)
        def _():
            chain(v, xout, xin, x_s, x_r, gx + 1).wait_send()

        @pl.when(gx > 0)
        def _():
            chain(v, xout_b, xin_b, b_s, b_r, gx - 1).wait_send()


def assemble(variables, rx, ctrl, field, row0, grow, axt, ending, out, stage):
    halves = out.shape[2] // LANES
    v = pl.program_id(0)
    for tile in range(field.shape[1] // 8):
        rows = slice(tile * 8, tile * 8 + 8)
        block = slice(tile * 8 * rx, (tile + 1) * 8 * rx)
        total = ending[rows, :]
        moved = jnp.zeros_like(total)
        for number in range(variables):
            part = total if number == 0 else pltpu.roll(total, LANES - number * rx, 1)
            moved = jnp.where(v == number, part, moved)
        ax = jnp.concatenate([axt[rows, :]] * halves, axis=1)
        entering = row0[rows, :]
        for x in range(rx)[::-1]:
            q = jnp.broadcast_to(moved[:, x:x + 1], (8, LANES))
            entering = ax * entering
            value = field[x, rows, :] + grow[rows, :] * jnp.concatenate([q] * halves, axis=1)
            value = value + entering
            for h in range(halves):
                stage[tile * halves + h, pl.ds(x, 8, stride=rx), :] = value[
                    :, h * LANES:(h + 1) * LANES
                ]
        for h in range(halves):
            lanes = slice(h * LANES, (h + 1) * LANES)
            out[0, block, lanes] = ctrl[0, block, lanes] + stage[tile * halves + h]


def body(
    control, background, vert_factor, length_rates, flash_weights, level_weights,
    obs_owner, obs_cell, obs_count, flash_obs, obs_error,
):
    variables, levels, rx, ry = control.shape
    nx, ny = lax.axis_size("gx"), lax.axis_size("gy")
    devices = nx * ny
    count = obs_cell.shape[0]
    vk = variables * levels
    step_x = length_rates[0] / (rx * nx)
    step_y = length_rates[1] / (ry * ny)
    gain = jnp.sqrt(jnp.expm1(-2.0 * step_x) * jnp.expm1(-2.0 * step_y))
    vmem = pl.BlockSpec(memory_space=pltpu.VMEM)
    dma = pltpu.SemaphoreType.DMA
    field, row0, grow, axt, ending, departure = pl.pallas_call(
        functools.partial(kernel, nx, ny, variables, levels, rx, ry),
        out_shape=(
            jax.ShapeDtypeStruct((rx, vk, ry), f32),
            jax.ShapeDtypeStruct((vk, ry), f32),
            jax.ShapeDtypeStruct((vk, ry), f32),
            jax.ShapeDtypeStruct((vk, LANES), f32),
            jax.ShapeDtypeStruct((levels, LANES), f32),
            jax.ShapeDtypeStruct((1, count), f32),
        ),
        in_specs=[vmem] + [pl.BlockSpec(memory_space=pltpu.HBM)] * 11,
        out_specs=(vmem,) * 6,
        scratch_shapes=[
            pltpu.VMEM((ry, 4 * rx), f32),
            pltpu.VMEM((devices, rx, ry), f32),
            pltpu.VMEM((devices, 8, count // 2), f32),
            pltpu.VMEM((ny, levels, LANES), f32),
            pltpu.VMEM((ny, levels, LANES), f32),
            pltpu.VMEM((levels, LANES), f32),
            pltpu.VMEM((variables, levels, ry), f32),
            pltpu.VMEM((variables, levels, ry), f32),
            pltpu.VMEM((variables, levels, ry), f32),
            pltpu.VMEM((variables, levels, ry), f32),
            pltpu.VMEM((variables * ry // LANES, 8 * rx, LANES), f32),
            pltpu.VMEM((rx, levels, ry), f32),
            pltpu.VMEM((2 * levels, vk), bf16),
            pltpu.VMEM((vk, 3 * levels), bf16),
            pltpu.VMEM((3 * variables + 1, levels, LANES), f32),
            pltpu.VMEM((16, LANES), f32),
            pltpu.VMEM((ry, ry), bf16),
            pltpu.VMEM((ry, ry), bf16),
            pltpu.VMEM((vk, ry), f32),
            pltpu.VMEM((rx, levels, ry), f32),
            pltpu.VMEM((rx, ry), f32),
            pltpu.VMEM((nx, levels, LANES), f32),
            pltpu.VMEM((nx, levels, LANES), f32),
            pltpu.VMEM((variables, levels * rx, ry), f32),
            pltpu.VMEM((variables, levels * rx, ry), f32),
            pltpu.VMEM((variables, levels, levels), f32),
            pltpu.VMEM((2, variables, levels), f32),
            pltpu.VMEM((variables, levels), f32),
            pltpu.VMEM((1, levels), f32),
            pltpu.VMEM((1, count), jnp.int32),
            pltpu.VMEM((1, count), jnp.int32),
            pltpu.VMEM((1, count), f32),
            pltpu.VMEM((1, count), f32),
            pltpu.VMEM((1, 1), jnp.int32),
            dma((10,)), dma((variables,)), dma((nx,)), dma((nx,)), dma((nx,)), dma((nx,)),
            dma((devices,)), dma((devices,)), dma((devices,)), dma((devices,)),
            dma((ny,)), dma((ny,)), dma((ny,)), dma((ny,)),
            dma((variables,)), dma((variables,)), dma((variables,)), dma((variables,)),
        ],
        compiler_params=pltpu.CompilerParams(
            collective_id=0, has_side_effects=True, vmem_limit_bytes=58 * 2**20
        ),
    )(
        gain, control.reshape(variables, levels * rx, ry),
        background.reshape(variables, levels * rx, ry),
        vert_factor, length_rates, flash_weights, level_weights[None], obs_owner.reshape(1, count),
        obs_cell[None], flash_obs[None], obs_error[None], obs_count[None],
    )
    cuts = 2
    deep = levels // cuts
    rows_at = lambda v, c: (v * cuts + c, 0)
    whole = pl.BlockSpec((1, deep * rx, ry), lambda v, c: (v, c, 0))
    grad = pl.pallas_call(
        functools.partial(assemble, variables, rx),
        grid=(variables, cuts),
        out_shape=jax.ShapeDtypeStruct((variables, levels * rx, ry), f32),
        in_specs=[
            whole,
            pl.BlockSpec((rx, deep, ry), lambda v, c: (0, v * cuts + c, 0)),
            pl.BlockSpec((deep, ry), rows_at),
            pl.BlockSpec((deep, ry), rows_at),
            pl.BlockSpec((deep, LANES), rows_at),
            pl.BlockSpec((deep, LANES), lambda v, c: (c, 0)),
        ],
        out_specs=whole,
        scratch_shapes=[pltpu.VMEM((deep // 8 * ry // LANES, 8 * rx, LANES), f32)],
        compiler_params=pltpu.CompilerParams(vmem_limit_bytes=58 * 2**20),
    )(control.reshape(variables, levels * rx, ry), field, row0, grow, axt, ending)
    return grad.reshape(control.shape), departure.reshape(count)


def solution(mesh):
    placed = (
        P(None, None, "gx", "gy"),
        P(None, None, "gx", "gy"),
        P(),
        P(),
        P(),
        P(),
        P(("gx", "gy"), None),
        P(("gx", "gy")),
        P(("gx", "gy")),
        P(("gx", "gy")),
        P(("gx", "gy")),
    )
    return jax.shard_map(
        body,
        mesh=mesh,
        in_specs=placed,
        out_specs=(P(None, None, "gx", "gy"), P(("gx", "gy"))),
        check_vma=False,
    )
```

```python
import functools
import jax
import jax.numpy as jnp
from jax import lax
from jax.experimental import pallas as pl
from jax.experimental.pallas import tpu as pltpu
from jax.sharding import PartitionSpec as P

LANES = 128
MESH = pl.DeviceIdType.MESH
f32, bf16 = jnp.float32, jnp.bfloat16


def split(value):
    high = value.astype(bf16)
    return high, (value - high.astype(f32)).astype(bf16)


def dot(left, right):
    return jnp.dot(left, right, preferred_element_type=f32)


def kernel(
    nx, ny, variables, levels, rx, ry,
    gain, ctrl_h, bg_h, vert_h, rate_h, flash_w_h, level_w_h, owner_h, cell_h, seen_h, error_h, live_h,
    out, dep,
    field, sums, sp_all, obs_all, edge, edge_b, q_ref, xin, xout, xin_b, xout_b, row0, axt, stage,
    base_levels, mstack, bstack, tab, raw, tri, tri_b, grow, fade, slopes, totals,
    qx, bx, ctrl, bg, vert, rate, flash_w, level_w, owner, cell, seen, error, live,
    in_s, ctrl_s, qx_s, qx_r, bx_s, bx_r,
    obs_s, obs_r, sp_s, sp_r, e_s, e_r, f_s, f_r, x_s, x_r, b_s, b_r,
):
    devices = nx * ny
    gx, gy = lax.axis_index("gx"), lax.axis_index("gy")
    me = gx * ny + gy
    halves = ry // LANES
    tiles = levels // 8
    vk = variables * levels
    lane = lax.broadcasted_iota(jnp.int32, (8, LANES), 1)
    small = [
        (vert_h, vert), (rate_h, rate), (flash_w_h, flash_w), (level_w_h, level_w),
        (owner_h, owner), (cell_h, cell), (seen_h, seen), (error_h, error), (live_h, live),
    ]
    small = [pltpu.make_async_copy(a, b, in_s.at[i + 1]) for i, (a, b) in enumerate(small)]
    bg_copy = pltpu.make_async_copy(bg_h, bg, in_s.at[0])
    ctrl_copy = [
        pltpu.make_async_copy(ctrl_h.at[v], ctrl.at[v], ctrl_s.at[v]) for v in range(variables)
    ]
    for copy in small + ctrl_copy + [bg_copy]:
        copy.start()

    def peer(offset):
        other = lax.rem(me + offset, devices)
        return (other // ny, lax.rem(other, ny))

    def to_all(ref, send, recv):
        def one(offset):
            return pltpu.make_async_remote_copy(
                ref.at[me], ref.at[me], send.at[offset], recv.at[me], peer(offset), MESH
            )
        return one

    def from_all(ref, send, recv, offset):
        src = lax.rem(me + offset, devices)
        return pltpu.make_async_remote_copy(
            ref.at[src], ref.at[src], send.at[offset], recv.at[src], peer(offset), MESH
        )

    def start_all(ref, send, recv):
        @pl.loop(1, devices)
        def _(offset):
            to_all(ref, send, recv)(offset).start()

    def wait_all(ref, send, recv):
        @pl.loop(1, devices)
        def _(offset):
            from_all(ref, send, recv, offset).wait_recv()
            to_all(ref, send, recv)(offset).wait_send()

    def row_copy(ref, send, recv, offset, slot):
        other = lax.rem(gy + offset, ny)
        return pltpu.make_async_remote_copy(
            ref.at[slot], ref.at[slot], send.at[offset], recv.at[slot], (gx, other), MESH
        )

    def start_row(ref, send, recv):
        @pl.loop(1, ny)
        def _(offset):
            row_copy(ref, send, recv, offset, gy).start()

    def wait_row(ref, send, recv):
        @pl.loop(1, ny)
        def _(offset):
            row_copy(ref, send, recv, offset, lax.rem(gy + offset, ny)).wait_recv()
            row_copy(ref, send, recv, offset, gy).wait_send()

    def chain(v, source, target, send, recv, other):
        return pltpu.make_async_remote_copy(
            source.at[v], target.at[v], send.at[v], recv.at[v], (other, gy), MESH
        )

    pitch = rx + 1

    def lay(slot, ref, v, tile, h):
        for k in range(8):
            stage[slot, k * pitch:k * pitch + rx, :] = ref[
                v, pl.ds((tile * 8 + k) * rx, rx), half(h)
            ]

    def half(h):
        return slice(h * LANES, (h + 1) * LANES)

    def rates(v, tile):
        rows = pl.ds(tile * 8, 8)
        return tab[v, rows, :], tab[variables + v, rows, :]

    barrier = pltpu.get_barrier_semaphore()

    @pl.loop(1, devices)
    def _(offset):
        pl.semaphore_signal(barrier, inc=1, device_id=peer(offset), device_id_type=MESH)
    for copy in small:
        copy.wait()

    count = seen.shape[1]
    per = count // 2
    where = cell[...].astype(f32)
    cell_x = jnp.floor(where * (1.0 / ry))
    cell_y = where - cell_x * ry
    place = lax.broadcasted_iota(jnp.int32, (1, count), 1)
    key = jnp.where(place < live[...], owner[...].astype(f32) * rx + cell_x, -1.0)
    flash = seen[...]
    weight = 1.0 / (error[...] * error[...])
    for number, value in enumerate((key, cell_y, weight, flash * weight)):
        for part in range(2):
            obs_all[me, 2 * number + part:2 * number + part + 1, :] = value[
                :, part * per:(part + 1) * per
            ]

    raw[...] = jnp.zeros_like(raw)
    raw[:variables, :levels] = rate[0] * (1.0 / (rx * nx))
    raw[variables:2 * variables, :levels] = rate[1] * (1.0 / (ry * ny))
    raw[2 * variables:3 * variables, :levels] = flash_w[...]
    raw[3 * variables:3 * variables + 1, :levels] = level_w[...]
    turned = raw[...].T
    for c in range(3 * variables + 1):
        tab[c] = jnp.broadcast_to(turned[:levels, c:c + 1], (levels, LANES))

    for v in range(variables):
        mine = slice(v * levels, (v + 1) * levels)
        scaled = vert[v] * gain[v:v + 1, :] * tab[2 * variables + v, :, :levels]
        high, low = split(scaled)
        mstack[:levels, mine] = high
        mstack[levels:, mine] = low
        high, low = split((scaled * tab[3 * variables, :, :levels]).T)
        bstack[mine, :levels] = high
        bstack[mine, levels:2 * levels] = high
        bstack[mine, 2 * levels:] = low
    down = lax.broadcasted_iota(jnp.int32, (ry, ry), 0)
    across = lax.broadcasted_iota(jnp.int32, (ry, ry), 1)
    tri[...] = jnp.where(down <= across, 1.0, 0.0).astype(bf16)
    tri_b[...] = jnp.where(down >= across, 1.0, 0.0).astype(bf16)

    def prefix(value, triangle):
        high, low = split(value)
        both = dot(jnp.concatenate([high, low], axis=0), triangle[...])
        return both[:value.shape[0]] + both[value.shape[0]:]

    wide = lambda value: jnp.concatenate([value] * halves, axis=1)
    position = lax.broadcasted_iota(jnp.int32, (8, ry), 1).astype(f32)

    edge[gy] = jnp.zeros((levels, LANES), f32)
    bx[gx] = jnp.zeros((levels, LANES), f32)

    @pl.when(gx == 0)
    def _():
        xin[...] = jnp.zeros_like(xin)

    @pl.when(gx == nx - 1)
    def _():
        xin_b[...] = jnp.zeros_like(xin_b)

    def step(slot, lag, last, next_x, own, source, target, send, recv):
        v = slot - lag

        @pl.when((v >= 0) & (v < variables))
        def _():
            @pl.when(lag > 0)
            def _():
                chain(v, source, target, send, recv, gx).wait_recv()

            @pl.when(lag < last)
            def _():
                source[v] = own(pl.ds(v * levels, levels)) + wide(
                    jnp.exp(-tab[v] * rx)
                ) * target[v]
                chain(v, source, target, send, recv, next_x).start()

    def step_forward(slot):
        step(slot, gx, nx - 1, gx + 1, lambda rows: field[rx - 1, rows, :], xout, xin, x_s, x_r)

    def step_back(slot):
        step(slot, nx - 1 - gx, nx - 1, gx - 1, lambda rows: row0[rows, :], xout_b, xin_b, b_s, b_r)

    slots = variables + nx - 1

    def corner(ref, send, recv, other, slot):
        return pltpu.make_async_remote_copy(
            ref.at[slot], ref.at[slot], send.at[other], recv.at[slot], (other, gy), MESH
        )

    def start_corner(ref, send, recv, ahead):
        for other in range(nx):
            @pl.when(ahead(gx, other))
            def _():
                corner(ref, send, recv, other, gx).start()

    def wait_corner(ref, send, recv, ahead):
        for other in range(nx):
            @pl.when(ahead(other, gx))
            def _():
                corner(ref, send, recv, other, other).wait_recv()

            @pl.when(ahead(gx, other))
            def _():
                corner(ref, send, recv, other, gx).wait_send()

    later, sooner = lambda a, b: b > a, lambda a, b: b < a
    inner = lax.rem(lane, rx)

    def scan_x(total, sx):
        s = 1
        while s < rx:
            total = total + jnp.where(inner >= s, jnp.exp(-sx * s), 0.0) * pltpu.roll(total, s, 1)
            s *= 2
        return total

    def rates_in_lanes(tile):
        both = [jnp.zeros((8, LANES), f32)] * 2
        for v in range(variables):
            here = (lane >= v * rx) & (lane < (v + 1) * rx)
            both = [jnp.where(here, new, old) for new, old in zip(rates(v, tile), both)]
        return both

    for v in range(variables):
        ctrl_copy[v].wait()

        @pl.loop(0, tiles // 2)
        def _(pair):
            parts, falls, decays = [], [], []
            for k in range(2):
                tile = pair * 2 + k
                rows = pl.ds(v * levels + tile * 8, 8)
                sx, sy = rates(v, tile)
                up, fall = jnp.exp(wide(sy) * position), jnp.exp(-wide(sy) * position)
                grow[rows, :], fade[rows, :] = up, fall
                ax = jnp.exp(-sx)
                axt[rows, :] = ax
                falls.append(fall)
                decays.append(wide(ax))
                for h in range(halves):
                    lay(k * halves + h, ctrl, v, tile, h)
                for x in range(rx):
                    strips = [
                        stage[k * halves + h, pl.ds(x, 8, stride=pitch), :] for h in range(halves)
                    ]
                    parts.append(jnp.concatenate(strips, axis=1) * up)
            parts = prefix(jnp.concatenate(parts, axis=0), tri)
            for k in range(2):
                tile = pair * 2 + k
                rows = pl.ds(v * levels + tile * 8, 8)
                state = jnp.zeros((8, ry), f32)
                column = edge[gy, pl.ds(tile * 8, 8), :]
                for x in range(rx):
                    at = (k * rx + x) * 8
                    part = parts[at:at + 8] * falls[k]
                    last = jnp.broadcast_to(part[:, ry - 1:], (8, LANES))
                    column = jnp.where(lane == v * rx + x, last, column)
                    state = decays[k] * state + part
                    field[x, rows, :] = state
                edge[gy, pl.ds(tile * 8, 8), :] = column

        if v == 0:
            pl.semaphore_wait(barrier, devices - 1)
            start_all(obs_all, obs_s, obs_r)
        if v == variables - 1:
            start_row(edge, e_s, e_r)
        step_forward(v)

    bg_copy.wait()

    @pl.loop(0, tiles)
    def _(tile):
        for v in range(variables):
            for h in range(halves):
                lay(v * halves + h, bg, v, tile, h)
        weights = [tab[2 * variables + v, pl.ds(tile * 8, 8), :] for v in range(variables)]
        for x in range(rx):
            for h in range(halves):
                part = jnp.zeros((8, LANES), f32)
                for v in range(variables):
                    part = part + weights[v] * stage[v * halves + h, pl.ds(x, 8, stride=pitch), :]
                base_levels[x, pl.ds(tile * 8, 8), half(h)] = part

    step_forward(variables)
    wait_all(obs_all, obs_s, obs_r)
    sums[...] = jnp.zeros_like(sums)
    row_x = lax.broadcasted_iota(jnp.int32, (rx, per), 0).astype(f32)
    row_y = lax.broadcasted_iota(jnp.int32, (ry, per), 0).astype(f32)
    base = (me * rx).astype(f32)

    @pl.loop(0, devices, unroll=2)
    def _(src):
        pieces, rights = [], []
        for part in range(2):
            hit = row_x == obs_all[src, part:part + 1, :] - base
            spot = obs_all[src, 2 + part:3 + part, :]
            rows = []
            for field_of in (4, 6):
                load = obs_all[src, field_of + part:field_of + part + 1, :]
                rows += split(jnp.where(hit, load, 0.0))
            pieces.append(jnp.concatenate(rows, axis=0))
            rights.append(jnp.where(row_y == spot, 1.0, 0.0).astype(bf16))
        sums[...] += lax.dot_general(
            jnp.concatenate(rights, axis=1), jnp.concatenate(pieces, axis=1),
            (((1,), (1,)), ((), ())), preferred_element_type=f32,
        )

    gathered = sums[...].T
    s1 = gathered[:rx] + gathered[rx:2 * rx]
    s2 = gathered[2 * rx:3 * rx] + gathered[3 * rx:]

    step_forward(variables + 1)
    wait_row(edge, e_s, e_r)

    @pl.loop(0, tiles)
    def _(tile):
        rows = pl.ds(tile * 8, 8)
        sx, sy = rates_in_lanes(tile)
        total = jnp.zeros((8, LANES), f32)
        for src in range(ny):
            far = jnp.maximum(gy - 1 - src, 0).astype(f32) * ry
            total = total + jnp.where(src < gy, jnp.exp(-sy * far) * edge[src, rows, :], 0.0)
        q_ref[rows, :] = total
        qx[gx, rows, :] = scan_x(total, sx)

    start_corner(qx, qx_s, qx_r, later)
    for slot in range(variables + 2, slots):
        step_forward(slot)
    wait_corner(qx, qx_s, qx_r, later)

    @pl.loop(0, tiles)
    def _(tile):
        rows = pl.ds(tile * 8, 8)
        sx, sy = rates_in_lanes(tile)
        total = jnp.zeros((8, LANES), f32)
        for src in range(nx):
            far = jnp.maximum(gx - 1 - src, 0).astype(f32) * rx
            total = total + jnp.where(src < gx, jnp.exp(-sx * far) * qx[src, rows, :], 0.0)
        total = jnp.exp(-sx) * pltpu.roll(total, LANES - (rx - 1), 1)
        total = q_ref[rows, :] + jnp.where(inner == 0, total, 0.0)
        q_ref[rows, :] = scan_x(total, sx) * jnp.exp(-sy)

    for v in range(variables):
        @pl.loop(0, tiles, unroll=2)
        def _(tile):
            rows = pl.ds(tile * 8, 8)
            mine = pl.ds(v * levels + tile * 8, 8)
            reach = fade[mine, :]
            q_all = q_ref[rows, :]
            ax = wide(axt[mine, :])
            entering = xin[v, rows, :]
            for x in range(rx):
                q = jnp.broadcast_to(q_all[:, v * rx + x:v * rx + x + 1], (8, LANES))
                entering = ax * entering
                field[x, mine, :] = field[x, mine, :] + reach * wide(q) + entering

    def soft_and_slope(value):
        small = jnp.exp(-jnp.abs(value))
        soft = jnp.maximum(value, 0.0) + jnp.log1p(small)
        return soft, jnp.where(value >= 0, 1.0, small) / (1.0 + small)

    @pl.loop(0, rx, unroll=4)
    def _(x):
        high, low = split(field[x])
        both = dot(mstack[...], high)
        value = both[:levels] + both[levels:] + dot(mstack[:levels, :], low) + base_levels[x]
        soft, slope = soft_and_slope(value)
        slopes[x] = slope
        totals[pl.ds(x, 1), :] = jnp.sum(wide(tab[3 * variables]) * soft, axis=0, keepdims=True)

    sp, sg = soft_and_slope(totals[...])
    sp_all[me] = sp
    totals[...] = sg * (sp * s1 - s2)
    start_all(sp_all, sp_s, sp_r)
    row0[...] = jnp.zeros_like(row0)

    @pl.loop(0, rx, unroll=4)
    def _(i):
        x = rx - 1 - i
        high, low = split(totals[pl.ds(x, 1), :] * slopes[x])
        back = dot(bstack[...], jnp.concatenate([high, low, high], axis=0))
        now = wide(axt[...]) * row0[...] + back
        row0[...] = now
        field[x] = now

    for v in range(variables):
        mine = slice(v * levels, (v + 1) * levels)

        @pl.loop(0, rx // 4)
        def _(group):
            lag, lead = fade[mine, :][None], grow[mine, :][None]
            value = field[pl.ds(group * 4, 4), mine, :] * lag
            value = prefix(value.reshape(4 * levels, ry), tri_b).reshape(4, levels, ry)
            field[pl.ds(group * 4, 4), mine, :] = value * lead

        @pl.loop(0, tiles, unroll=2)
        def _(tile):
            rows = pl.ds(tile * 8, 8)
            here = pl.ds(v * levels + tile * 8, 8)
            column = bx[gx, rows, :]
            for x in range(rx):
                own = field[x, here, :LANES][:, :1]
                column = jnp.where(lane == v * rx + x, jnp.broadcast_to(own, (8, LANES)), column)
            bx[gx, rows, :] = column

        if v == variables - 1:
            start_corner(bx, bx_s, bx_r, sooner)
        step_back(v)

    wait_corner(bx, bx_s, bx_r, sooner)

    @pl.loop(0, tiles)
    def _(tile):
        rows = pl.ds(tile * 8, 8)
        sx, sy = rates_in_lanes(tile)
        total = jnp.zeros((8, LANES), f32)
        for src in range(nx):
            far = jnp.maximum(src - gx - 1, 0).astype(f32) * rx
            total = total + jnp.where(src > gx, jnp.exp(-sx * far) * bx[src, rows, :], 0.0)
        total = jnp.where(inner == 0, total, 0.0)
        s = 1
        while s < rx:
            total = total + jnp.where((inner >= s) & (inner < 2 * s), pltpu.roll(total, s, 1), 0.0)
            s *= 2
        edge_b[gy, rows, :] = bx[gx, rows, :] + jnp.exp(-sx * (rx - inner).astype(f32)) * total

    start_row(edge_b, f_s, f_r)
    step_back(variables)
    wait_all(sp_all, sp_s, sp_r)
    column_y = lax.broadcasted_iota(jnp.int32, (ry, count), 0).astype(f32)
    pick = jnp.where(column_y == cell_y, 1.0, 0.0).astype(bf16)
    batch = 8
    row_of = lax.broadcasted_iota(jnp.int32, (batch * rx, count), 0).astype(f32)

    def find(group, found):
        high, low = split(sp_all[pl.ds(group * batch, batch)].reshape(batch * rx, ry))
        value = dot(jnp.concatenate([high, low], axis=0), pick)
        value = value[:batch * rx] + value[batch * rx:]
        hit = row_of == key - (group * (batch * rx)).astype(f32)
        return found + jnp.sum(jnp.where(hit, value, 0.0).reshape(-1, 8, count), axis=0)

    found = lax.fori_loop(0, devices // batch, find, jnp.zeros((8, count), f32))
    found = jnp.sum(found, axis=0, keepdims=True)
    dep[...] = jnp.where(key >= 0, found - flash, 0.0)

    for slot in range(variables + 1, slots):
        step_back(slot)
    entered = xin_b[...].reshape(vk, ry) * fade[...]
    row0[...] = prefix(entered, tri_b) * grow[...]
    wait_row(edge_b, f_s, f_r)

    @pl.loop(0, tiles)
    def _(tile):
        rows = pl.ds(tile * 8, 8)
        sx, sy = rates_in_lanes(tile)
        total = jnp.zeros((8, LANES), f32)
        for src in range(ny):
            far = jnp.maximum(src - gy - 1, 0).astype(f32) * ry
            total = total + jnp.where(src > gy, jnp.exp(-sy * far) * edge_b[src, rows, :], 0.0)
        total = total * jnp.exp(-sy * ry)
        for v in range(variables):
            mine = pl.ds(v * levels + tile * 8, 8)
            reach = grow[mine, :]
            ax = wide(axt[mine, :])
            entering = row0[mine, :]
            for x in range(rx)[::-1]:
                q = jnp.broadcast_to(total[:, v * rx + x:v * rx + x + 1], (8, LANES))
                entering = ax * entering
                value = field[x, mine, :] + reach * wide(q) + entering
                for h in range(halves):
                    stage[v * halves + h, pl.ds(x, 8, stride=pitch), :] = value[:, half(h)]
            for h in range(halves):
                for k in range(8):
                    at = (v, pl.ds((tile * 8 + k) * rx, rx), half(h))
                    out[at] = ctrl[at] + stage[v * halves + h, k * pitch:k * pitch + rx, :]

    for v in range(variables):
        @pl.when(gx < nx - 1)
        def _():
            chain(v, xout, xin, x_s, x_r, gx + 1).wait_send()

        @pl.when(gx > 0)
        def _():
            chain(v, xout_b, xin_b, b_s, b_r, gx - 1).wait_send()


def body(
    control, background, vert_factor, length_rates, flash_weights, level_weights,
    obs_owner, obs_cell, obs_count, flash_obs, obs_error,
):
    variables, levels, rx, ry = control.shape
    nx, ny = lax.axis_size("gx"), lax.axis_size("gy")
    devices = nx * ny
    count = obs_cell.shape[0]
    vk = variables * levels
    step_x = length_rates[0] / (rx * nx)
    step_y = length_rates[1] / (ry * ny)
    gain = jnp.sqrt(jnp.expm1(-2.0 * step_x) * jnp.expm1(-2.0 * step_y))
    vmem = pl.BlockSpec(memory_space=pltpu.VMEM)
    dma = pltpu.SemaphoreType.DMA
    grad, departure = pl.pallas_call(
        functools.partial(kernel, nx, ny, variables, levels, rx, ry),
        out_shape=(
            jax.ShapeDtypeStruct((variables, levels * rx, ry), f32),
            jax.ShapeDtypeStruct((1, count), f32),
        ),
        in_specs=[vmem] + [pl.BlockSpec(memory_space=pltpu.HBM)] * 11,
        out_specs=(vmem, vmem),
        scratch_shapes=[
            pltpu.VMEM((rx, vk, ry), f32),
            pltpu.VMEM((ry, 4 * rx), f32),
            pltpu.VMEM((devices, rx, ry), f32),
            pltpu.VMEM((devices, 8, count // 2), f32),
            pltpu.VMEM((ny, levels, LANES), f32),
            pltpu.VMEM((ny, levels, LANES), f32),
            pltpu.VMEM((levels, LANES), f32),
            pltpu.VMEM((variables, levels, ry), f32),
            pltpu.VMEM((variables, levels, ry), f32),
            pltpu.VMEM((variables, levels, ry), f32),
            pltpu.VMEM((variables, levels, ry), f32),
            pltpu.VMEM((vk, ry), f32),
            pltpu.VMEM((vk, LANES), f32),
            pltpu.VMEM((variables * ry // LANES, 8 * rx + 8, LANES), f32),
            pltpu.VMEM((rx, levels, ry), f32),
            pltpu.VMEM((2 * levels, vk), bf16),
            pltpu.VMEM((vk, 3 * levels), bf16),
            pltpu.VMEM((3 * variables + 1, levels, LANES), f32),
            pltpu.VMEM((16, LANES), f32),
            pltpu.VMEM((ry, ry), bf16),
            pltpu.VMEM((ry, ry), bf16),
            pltpu.VMEM((vk, ry), f32),
            pltpu.VMEM((vk, ry), f32),
            pltpu.VMEM((rx, levels, ry), f32),
            pltpu.VMEM((rx, ry), f32),
            pltpu.VMEM((nx, levels, LANES), f32),
            pltpu.VMEM((nx, levels, LANES), f32),
            pltpu.VMEM((variables, levels * rx, ry), f32),
            pltpu.VMEM((variables, levels * rx, ry), f32),
            pltpu.VMEM((variables, levels, levels), f32),
            pltpu.VMEM((2, variables, levels), f32),
            pltpu.VMEM((variables, levels), f32),
            pltpu.VMEM((1, levels), f32),
            pltpu.VMEM((1, count), jnp.int32),
            pltpu.VMEM((1, count), jnp.int32),
            pltpu.VMEM((1, count), f32),
            pltpu.VMEM((1, count), f32),
            pltpu.VMEM((1, 1), jnp.int32),
            dma((10,)), dma((variables,)), dma((nx,)), dma((nx,)), dma((nx,)), dma((nx,)),
            dma((devices,)), dma((devices,)), dma((devices,)), dma((devices,)),
            dma((ny,)), dma((ny,)), dma((ny,)), dma((ny,)),
            dma((variables,)), dma((variables,)), dma((variables,)), dma((variables,)),
        ],
        compiler_params=pltpu.CompilerParams(
            collective_id=0, has_side_effects=True, vmem_limit_bytes=58 * 2**20
        ),
    )(
        gain, control.reshape(variables, levels * rx, ry),
        background.reshape(variables, levels * rx, ry),
        vert_factor, length_rates, flash_weights, level_weights[None], obs_owner.reshape(1, count),
        obs_cell[None], flash_obs[None], obs_error[None], obs_count[None],
    )
    return grad.reshape(control.shape), departure.reshape(count)


def solution(mesh):
    placed = (
        P(None, None, "gx", "gy"),
        P(None, None, "gx", "gy"),
        P(),
        P(),
        P(),
        P(),
        P(("gx", "gy"), None),
        P(("gx", "gy")),
        P(("gx", "gy")),
        P(("gx", "gy")),
        P(("gx", "gy")),
    )
    return jax.shard_map(
        body,
        mesh=mesh,
        in_specs=placed,
        out_specs=(P(None, None, "gx", "gy"), P(("gx", "gy"))),
        check_vma=False,
    )
```
